32 devices in a mesh: tm: 8 (over z, y), row: 4 (over x, core).
Axes of the slice: x: 2, y: 2, z: 4, core: 2. Of those that a mesh axis runs over, the one named last changes fastest.
Arguments:
- output_first_half: bfloat16 [16, 4, 64, 320], P('tm', 'row'), may hold values from -6 to 6
- y_second: bfloat16 [16, 4, 64, 320], P('tm', 'row'), may hold values from -6 to 6
- cot_first: bfloat16 [16, 4, 64, 320], P('tm', 'row'), may hold values from -6 to 6
- cot_second: bfloat16 [16, 4, 64, 320], P('tm', 'row'), may hold values from -6 to 6
- weight_space: bfloat16 [3, 3, 2, 160, 160], replicated, may hold values from -0.15625 to 0.15625
- temporal_weight: bfloat16 [3, 5, 128, 128], replicated, may hold values from -0.3125 to 0.3125
Outputs:
- x_first: bfloat16 [16, 4, 64, 320], P('tm', 'row')
- x_second: bfloat16 [16, 4, 64, 320], P('tm', 'row')
- grad_first: bfloat16 [16, 4, 64, 320], P('tm', 'row')
- grad_second: bfloat16 [16, 4, 64, 320], P('tm', 'row')
- spatial_weight_gradient: float32 [460800], P(('tm', 'row'))
- grad_time: float32 [245760], P(('tm', 'row'))
The draws below stay inside these ranges and needn't reach their ends.
All inputs are finite; a program needn't handle non-finite values.
Results may differ from the reference program's by a relative error of at most 0.007.
Values may be sent and summed in bfloat16 or wider, within the bound.
No kernel may reach another device: no remote copies, remote signals or barrier semaphores. Data moves between devices by JAX's collectives and lax.ppermute only.
A program may use at most 64 MiB of HBM per device.

```python
import math
import jax
import jax.numpy as jnp
from jax import lax

CH = 320
GS = 160
GROUP_CHANNELS = 128
WIDTH = 64
FRAMES = 16
ROWS = 4
CELLS_ALL = 4096
GRS = 2
TEMPORAL_GROUPS = 5


def steps_of(own_key, shape, cuts, low, largest):
    def one(position, blocks):
        heights = jax.random.uniform(jax.random.fold_in(jax.random.fold_in(own_key, 6), position), (blocks,), jnp.float32, low / len(cuts), largest / len(cuts))
        return jnp.repeat(jnp.exp(heights), shape[position] // blocks).reshape((-1,) + (1,) * (len(shape) - position - 1))

    factor_of = one(*cuts[0])
    for cut in cuts[1:]:
        factor_of = factor_of * one(*cut)
    return factor_of


def centred(rng, extent, scale, reach, cuts=(), held_as=jnp.bfloat16):
    array = jax.random.normal(rng, extent, jnp.float32) * scale
    if len(cuts) > 0:
        array = steps_of(rng, extent, cuts, -0.22, 0.18) * array
    return jnp.clip(array, min=-reach, max=reach).astype(held_as)


def setup_inputs(seed: int = 0) -> dict:
    key_list = jax.random.split(jax.random.key(seed), 7)
    return {
        "output_first_half": centred(key_list[0], (FRAMES, ROWS, WIDTH, CH), 1.0, 6.0, ((0, 8), (1, 4))),
        "y_second": centred(key_list[1], (FRAMES, ROWS, WIDTH, CH), 1.0, 6.0, ((0, 8), (1, 4))),
        "cot_first": centred(key_list[2], (FRAMES, ROWS, WIDTH, CH), 1.0, 6.0, ((0, 8), (1, 4))),
        "cot_second": centred(key_list[3], (FRAMES, ROWS, WIDTH, CH), 1.0, 6.0, ((0, 8), (1, 4))),
        "weight_space": centred(key_list[4], (3, 3, GRS, GS, GS), (9 * GS) ** -0.5, 0.15625),
        "temporal_weight": centred(key_list[5], (3, TEMPORAL_GROUPS, GROUP_CHANNELS, GROUP_CHANNELS), (3 * GROUP_CHANNELS) ** -0.5, 0.3125),
    }


HAAR = 0.7071067811865476

def haar_pair_squeeze(input_frames):
    even_frames = input_frames[0::2].astype(jnp.float32)
    odd_frames = input_frames[1::2].astype(jnp.float32)
    return jnp.concatenate([(even_frames + odd_frames) * HAAR, (even_frames - odd_frames) * HAAR], axis=-1)

def unsqueeze_pairs(packed):
    half_ch = packed.shape[-1] // 2
    low_band = packed[..., :half_ch]
    high_band = packed[..., half_ch:]
    stacked = jnp.stack([(low_band + high_band) * HAAR, (low_band - high_band) * HAAR], axis=1)
    return stacked.reshape((2 * low_band.shape[0],) + low_band.shape[1:])

def silu_slope(values):
    sigmoid_v = jax.nn.sigmoid(values)
    return sigmoid_v * (1.0 + values * (1.0 - sigmoid_v))

def split_groups(tensor, groups):
    return tensor.reshape(tensor.shape[:-1] + (groups, tensor.shape[-1] // groups))

def merge_groups(tensor):
    return tensor.reshape(tensor.shape[:-2] + (tensor.shape[-2] * tensor.shape[-1],))

def time_apply(act_ext, temporal_weight):
    length = act_ext.shape[0] - 2
    groups = temporal_weight.shape[1]
    summed = None
    for offset in range(3):
        window = split_groups(act_ext[offset:offset + length].astype(jnp.float32), groups)
        partial_sum = jnp.einsum('t...gi,gio->t...go', window, temporal_weight[offset].astype(jnp.float32))
        summed = partial_sum if summed is None else summed + partial_sum
    return merge_groups(summed)

def time_back(cot_ext, temporal_weight):
    length = cot_ext.shape[0] - 2
    groups = temporal_weight.shape[1]
    summed = None
    for offset in range(3):
        window = split_groups(cot_ext[2 - offset:2 - offset + length].astype(jnp.float32), groups)
        partial_sum = jnp.einsum('t...go,gio->t...gi', window, temporal_weight[offset].astype(jnp.float32))
        summed = partial_sum if summed is None else summed + partial_sum
    return merge_groups(summed)

def time_wgrad(act_ext, cot_inner, groups):
    length = cot_inner.shape[0]
    cot_split = split_groups(cot_inner.astype(jnp.float32), groups)
    result = []
    for offset in range(3):
        window = split_groups(act_ext[offset:offset + length].astype(jnp.float32), groups)
        result.append(jnp.einsum('t...gi,t...go->gio', window, cot_split))
    return jnp.stack(result)

def time_core(y_ext, cot_ext, temporal_weight):
    squeezed = haar_pair_squeeze(y_ext)
    act_time = jax.nn.silu(squeezed).astype(jnp.bfloat16)
    temporal_cotangent = haar_pair_squeeze(cot_ext).astype(jnp.bfloat16)
    branch_time = unsqueeze_pairs(time_apply(act_time, temporal_weight)).astype(jnp.bfloat16)
    back_sum = time_back(temporal_cotangent, temporal_weight) * silu_slope(squeezed[1:-1])
    back_time = unsqueeze_pairs(back_sum).astype(jnp.bfloat16)
    sum_time = time_wgrad(act_time, temporal_cotangent[1:-1], temporal_weight.shape[1])
    return (branch_time, back_time, sum_time)

def space_apply(act_pad, weight_space):
    rows_in = act_pad.shape[-3] - 2
    cols_in = act_pad.shape[-2] - 2
    groups = weight_space.shape[2]
    summed = None
    for row_tap in range(3):
        for col_tap in range(3):
            window = act_pad[..., row_tap:row_tap + rows_in, col_tap:col_tap + cols_in, :]
            window = split_groups(window.astype(jnp.float32), groups)
            partial_sum = jnp.einsum('...gi,gio->...go', window, weight_space[row_tap, col_tap].astype(jnp.float32))
            summed = partial_sum if summed is None else summed + partial_sum
    return merge_groups(summed)

def space_back(cot_pad, weight_space):
    rows_in = cot_pad.shape[-3] - 2
    cols_in = cot_pad.shape[-2] - 2
    groups = weight_space.shape[2]
    summed = None
    for row_tap in range(3):
        for col_tap in range(3):
            window = cot_pad[..., 2 - row_tap:2 - row_tap + rows_in, 2 - col_tap:2 - col_tap + cols_in, :]
            window = split_groups(window.astype(jnp.float32), groups)
            partial_sum = jnp.einsum('...go,gio->...gi', window, weight_space[row_tap, col_tap].astype(jnp.float32))
            summed = partial_sum if summed is None else summed + partial_sum
    return merge_groups(summed)

def space_wgrad(act_pad, cot_inner, groups):
    rows_in = cot_inner.shape[-3]
    cols_in = cot_inner.shape[-2]
    cot_split = split_groups(cot_inner.astype(jnp.float32), groups)
    result = []
    for row_tap in range(3):
        row_list = []
        for col_tap in range(3):
            window = act_pad[..., row_tap:row_tap + rows_in, col_tap:col_tap + cols_in, :]
            window = split_groups(window.astype(jnp.float32), groups)
            row_list.append(jnp.einsum('...gi,...go->gio', window, cot_split))
        result.append(jnp.stack(row_list))
    return jnp.stack(result)

def reference(output_first_half, y_second, cot_first, cot_second, weight_space, temporal_weight):
    frame_pad = ((2, 2), (0, 0), (0, 0))

    def time_row(carry, inputs):
        row_y, row_cot = inputs
        branch_time, back_time, sum_time = time_core(jnp.pad(row_y, frame_pad), jnp.pad(row_cot, frame_pad), temporal_weight)
        return (carry + sum_time, (branch_time, back_time))
    init_time = jnp.zeros(temporal_weight.shape, jnp.float32)
    sum_time, (branch_rows, back_rows) = lax.scan(time_row, init_time, (jnp.swapaxes(output_first_half, 0, 1), jnp.swapaxes(cot_second, 0, 1)))
    branch_time = jnp.swapaxes(branch_rows, 0, 1)
    back_time = jnp.swapaxes(back_rows, 0, 1)
    space_pad = ((1, 1), (1, 1), (0, 0))

    def space_frame(carry, inputs):
        frame_y1, frame_y2, frame_c1, frame_c2, frame_branch, frame_back = inputs
        recovered = (frame_y2.astype(jnp.float32) - frame_branch.astype(jnp.float32)).astype(jnp.bfloat16)
        first_grad = (frame_c1.astype(jnp.float32) + frame_back.astype(jnp.float32)).astype(jnp.bfloat16)
        act_pad = jax.nn.silu(jnp.pad(recovered, space_pad).astype(jnp.float32)).astype(jnp.bfloat16)
        first_rec = (frame_y1.astype(jnp.float32) - space_apply(act_pad, weight_space)).astype(jnp.bfloat16)
        back_sum = space_back(jnp.pad(first_grad, space_pad), weight_space) * silu_slope(recovered.astype(jnp.float32))
        second_grad = (frame_c2.astype(jnp.float32) + back_sum).astype(jnp.bfloat16)
        return (carry + space_wgrad(act_pad, first_grad, weight_space.shape[2]), (first_rec, recovered, first_grad, second_grad))
    init_space = jnp.zeros(weight_space.shape, jnp.float32)
    sum_space, outs = lax.scan(space_frame, init_space, (output_first_half, y_second, cot_first, cot_second, branch_time, back_time))
    x_first, x_second, grad_first, grad_second = outs
    factor = 1.0 / math.sqrt(CELLS_ALL)
    return (x_first, x_second, grad_first, grad_second, sum_space.reshape(-1) * factor, sum_time.reshape(-1) * factor)
```

```python
import functools
import math

import jax
import jax.numpy as jnp
from jax import lax
from jax.experimental import pallas as pl
from jax.experimental.pallas import tpu as pltpu
from jax.sharding import PartitionSpec as P

HAAR = 0.7071067811865476
LANES = 128
F32 = jnp.float32
BF16 = jnp.bfloat16


def round_up(value, unit):
    return (value + unit - 1) // unit * unit


def on_device(body, args, outs, scratch=(), flops=0):
    whole = pl.BlockSpec(memory_space=pltpu.VMEM)
    moved = sum(math.prod(a.shape) * a.dtype.itemsize for a in (*args, *outs))
    return pl.pallas_call(
        body,
        out_shape=outs,
        in_specs=[whole] * len(args),
        out_specs=[whole] * len(outs),
        scratch_shapes=list(scratch),
        compiler_params=pltpu.CompilerParams(vmem_limit_bytes=40 * 1024 * 1024),
        cost_estimate=pl.CostEstimate(flops=flops, bytes_accessed=moved, transcendentals=0),
    )(*args)


def shape(dims, dtype):
    return jax.ShapeDtypeStruct(tuple(dims), dtype)


def sigmoid(v):
    return 1.0 / (1.0 + jnp.exp(-v))


def silu_slope(v):
    s = sigmoid(v)
    return s * (1.0 + v * (1.0 - s))


def dot(left, right, left_dim, right_dim):
    return lax.dot_general(
        left, right, (((left_dim,), (right_dim,)), ((), ())), preferred_element_type=F32
    )


def squeezed(ref):
    even, odd = ref[0, 0].astype(F32), ref[1, 0].astype(F32)
    return jnp.concatenate([(even + odd) * HAAR, (even - odd) * HAAR], axis=-1)


def unsqueezed(packed):
    half = packed.shape[-1] // 2
    low, high = packed[:, :half], packed[:, half:]
    return (low + high) * HAAR, (low - high) * HAAR


def open_body(y_ref, cot_ref, out_ref):
    sq = squeezed(y_ref)
    cols = sq.shape[0]
    out_ref[:cols] = (sq * sigmoid(sq)).astype(BF16)
    out_ref[cols:] = squeezed(cot_ref).astype(BF16)


def time_body(own, before, after, y1, y2, c1, weight, x2_out, g1_out, packed_out):
    cols, ch = y2.shape[2:]
    groups, width = weight.shape[1:3]
    forth, back = [], []
    for q in range(groups):
        lanes = slice(q * width, (q + 1) * width)
        forth.append(
            dot(before[:cols, lanes], weight[0, q], 1, 0)
            + dot(own[:cols, lanes], weight[1, q], 1, 0)
            + dot(after[:cols, lanes], weight[2, q], 1, 0)
        )
        back.append(
            dot(after[cols:, lanes], weight[0, q], 1, 1)
            + dot(own[cols:, lanes], weight[1, q], 1, 1)
            + dot(before[cols:, lanes], weight[2, q], 1, 1)
        )
    branch = unsqueezed(jnp.concatenate(forth, axis=-1))
    back = unsqueezed(jnp.concatenate(back, axis=-1) * silu_slope(squeezed(y1)))
    frames = []
    for f in range(2):
        x2 = (y2[f, 0].astype(F32) - branch[f].astype(BF16).astype(F32)).astype(BF16)
        g1 = (c1[f, 0].astype(F32) + back[f].astype(BF16).astype(F32)).astype(BF16)
        x2_out[f, 0] = x2
        g1_out[f, 0] = g1
        v = x2.astype(F32)
        frames.append(jnp.concatenate([v * sigmoid(v), g1.astype(F32)], axis=-1))
    packed_out[...] = jnp.concatenate(frames, axis=0).T.astype(BF16)


def time_terms(own, before, after, total):
    cols = own.shape[0] // 2
    width = total.shape[1]
    groups = own.shape[1] // width
    for k, ref in enumerate((before, own, after)):
        for q in range(groups):
            lanes = slice(q * width, (q + 1) * width)
            term = dot(ref[:cols, lanes].astype(F32).T.astype(BF16), own[cols:, lanes], 1, 0)
            total[pl.ds((k * groups + q) * width, width), :] = term


def time_sum_body(offsets, rows, own, before, after, keep, send, total):
    time_terms(own, before, after, total)
    me, peers, steps = lax.axis_index("row"), lax.axis_size("row"), lax.axis_size("tm")
    held = keep.shape[2]
    for u, offset in enumerate(offsets):
        for t in range(steps):
            mine = (t * peers + (me ^ offset)) * rows
            other = (t * peers + (me ^ offset ^ 1)) * rows
            keep[u, t] = total[pl.ds(mine, held), :]
            send[u, t] = total[pl.ds(other, held), :].astype(BF16)


def time_sum_whole_body(own, before, after, total):
    time_terms(own, before, after, total)


def fold_body(kept, came, keep, send):
    half = keep.shape[0]
    keep[...] = kept[:half] + came[:half].astype(F32)
    send[...] = (kept[half:] + came[half:].astype(F32)).astype(BF16)


def space_terms(slots, rows_ref, cols, store):
    peers = len(slots)
    me = lax.axis_index("row")
    for k, ref in enumerate(slots):
        rows_ref[me ^ k] = ref[...]
    ch = rows_ref.shape[1] // 2
    column = lax.broadcasted_iota(jnp.int32, (ch, LANES), 1) % cols
    act, shifts = [], ([], [], [])
    for r in range(peers):
        act.append(rows_ref[r, :ch])
        cot = rows_ref[r, ch:]
        wide = cot.astype(F32)
        later = jnp.where(column == cols - 1, 0.0, pltpu.roll(wide, LANES - 1, 1))
        sooner = jnp.where(column == 0, 0.0, pltpu.roll(wide, 1, 1))
        for held, value in zip(shifts, (later.astype(BF16), cot, sooner.astype(BF16))):
            held.append(value)
    for a in range(3):
        pairs = [(r, r - a + 1) for r in range(peers) if 0 <= r - a + 1 < peers]
        left = jnp.concatenate([act[r] for r, _ in pairs], axis=1)
        for b in range(3):
            right = jnp.concatenate([shifts[b][r] for _, r in pairs], axis=1)
            store(a * 3 + b, left, right)


def segments(width):
    period = LANES // math.gcd(width, LANES)
    found = []
    for j in range(period * width // LANES):
        row, lane = [], 0
        while lane < LANES:
            at = j * LANES + lane
            source, column = divmod(at, width)
            tile, first = divmod(column, LANES)
            row.append((lane, source, tile, (lane - first) % LANES))
            lane += min(LANES - first, width - column, LANES - lane)
        found.append(row)
    return period, found


def space_sum_body(groups, rows, *refs):
    peers, steps = lax.axis_size("row"), lax.axis_size("tm")
    slots, (kept, came), refs = refs[:peers], refs[peers : peers + 2], refs[peers + 2 :]
    mine, sends, (rows_ref, main, rest) = refs[0], refs[1:steps], refs[steps:]
    ch = rows_ref.shape[1] // 2
    width = ch // groups

    def store(tap, left, right):
        for q in range(groups):
            part = slice(q * width, (q + 1) * width)
            term = dot(left[part], right[part], 1, 1)
            at = pl.ds((tap * groups + q) * width, width)
            main[at, :] = term[:, :LANES]
            rest[at, : width - LANES] = term[:, LANES:]

    space_terms(slots, rows_ref, LANES // 2, store)
    period, layout = segments(width)
    held = round_up(-(-rows // period), 8)
    lane = lax.broadcasted_iota(jnp.int32, (held, LANES), 1)
    here, me = lax.axis_index("tm"), lax.axis_index("row")
    early = kept.shape[2]
    for k in range(steps):
        t = here ^ k
        start = (t * peers + me) * rows
        rolled = {}

        def source(j, tile, amount):
            if (j, tile, amount) not in rolled:
                ref = (main, rest)[tile]
                value = ref[pl.ds(start + j, held, stride=period), :]
                rolled[j, tile, amount] = pltpu.roll(value, amount, 1) if amount else value
            return rolled[j, tile, amount]

        parts = [kept[0, t] + came[0, t].astype(F32)]
        for row in layout:
            value = None
            for first, j, tile, amount in row:
                piece = source(j, tile, amount)
                value = piece if value is None else jnp.where(lane < first, value, piece)
            parts.append(value)
        blank = mine.shape[0] - early - held * len(layout)
        if blank:
            parts.append(jnp.zeros((blank, LANES), F32))
        piece = jnp.concatenate(parts, axis=0)
        if k == 0:
            mine[...] = piece
        else:
            sends[k - 1][...] = piece.astype(BF16)


def space_sum_whole_body(groups, *refs):
    peers = lax.axis_size("row")
    slots, (total, rows_ref) = refs[:peers], refs[peers:]
    ch = rows_ref.shape[1] // 2
    width = ch // groups

    def store(tap, left, right):
        for q in range(groups):
            part = slice(q * width, (q + 1) * width)
            at = pl.ds((tap * groups + q) * width, width)
            total[at, :] = dot(left[part], right[part], 1, 1)

    space_terms(slots, rows_ref, LANES // 2, store)


def final_body(factor, early, period, stride, *refs):
    (mine, *came), (space_out, time_out) = refs[:-2], refs[-2:]
    total = mine[...]
    for ref in came:
        total = total + ref[...].astype(F32)
    total = total * factor
    time_out[...] = total[: time_out.shape[0]]
    held = space_out.shape[0] // stride
    tall = (total.shape[0] - early) // stride // 8 * 8
    for j in range(stride):
        first = early + j * tall
        space_out[pl.ds(j, held, stride=stride), :] = total[first : first + held]


def space_body(*refs):
    peers = lax.axis_size("row")
    slots, (y1, c2, x2, weight, x1_out, g2_out, rows_ref) = refs[:peers], refs[peers:]
    me = lax.axis_index("row")
    cols, ch = y1.shape[2:]
    groups, width = weight.shape[2:4]
    rows_ref[0] = jnp.zeros(rows_ref.shape[1:], BF16)
    rows_ref[peers + 1] = jnp.zeros(rows_ref.shape[1:], BF16)
    for k, ref in enumerate(slots):
        rows_ref[(me ^ k) + 1] = ref[...]
    column = lax.broadcasted_iota(jnp.int32, (LANES, width), 0) % cols
    forth, back = [None] * groups, [None] * groups
    for a in range(3):
        row = rows_ref[me + a].astype(F32).T
        for q in range(groups):
            for first, sums in ((0, forth), (ch, back)):
                value = row[:, first + q * width : first + (q + 1) * width]
                sooner = jnp.where(column == 0, 0.0, pltpu.roll(value, 1, 0))
                later = jnp.where(column == cols - 1, 0.0, pltpu.roll(value, LANES - 1, 0))
                for b, moved in enumerate((sooner, value, later)):
                    if first:
                        term = dot(moved.astype(BF16), weight[2 - a, 2 - b, q], 1, 1)
                    else:
                        term = dot(moved.astype(BF16), weight[a, b, q], 1, 0)
                    sums[q] = term if sums[q] is None else sums[q] + term
    forth = jnp.concatenate(forth, axis=-1)
    back = jnp.concatenate(back, axis=-1)
    for f in range(2):
        part = slice(f * cols, (f + 1) * cols)
        x1_out[f, 0] = (y1[f, 0].astype(F32) - forth[part]).astype(BF16)
        slope = silu_slope(x2[f, 0].astype(F32))
        g2_out[f, 0] = (c2[f, 0].astype(F32) + slope * back[part]).astype(BF16)


def swap(x, axis, bit):
    return lax.ppermute(x, axis, [(i, i ^ bit) for i in range(lax.axis_size(axis))])


def row_offsets(bits):
    if not bits:
        return [0]
    rest = row_offsets(bits[1:])
    return rest + [o ^ bits[0] for o in rest]


def per_device(y1, y2, c1, c2, weight_space, temporal_weight):
    steps, peers = lax.axis_size("tm"), lax.axis_size("row")
    devices = steps * peers
    frames, rows_here, cols, ch = y1.shape
    groups = weight_space.shape[2]
    width = ch // groups
    taps = weight_space.shape[0] * weight_space.shape[1]
    factor = 1.0 / math.sqrt(frames * rows_here * cols * devices)
    time_groups, time_width = temporal_weight.shape[1:3]
    time_rows = 3 * time_groups * time_width
    space_rows = taps * ch

    packed = on_device(open_body, (y1, c2), [shape((2 * cols, 2 * ch), BF16)])[0]
    up = [(i, i + 1) for i in range(steps - 1)]
    before = lax.ppermute(packed, "tm", up)
    after = lax.ppermute(packed, "tm", [(j, i) for i, j in up])
    x2, g1, held = on_device(
        time_body,
        (packed, before, after, y1, y2, c1, temporal_weight),
        [shape(y1.shape, BF16), shape(y1.shape, BF16), shape((2 * ch, 2 * cols), BF16)],
    )

    slots = {0: held}
    bits = [1 << i for i in range(peers.bit_length() - 1)]
    for bit in reversed(bits):
        for k in list(slots):
            slots[k ^ bit] = swap(slots[k], "row", bit)
    gathered = [slots[k] for k in range(peers)]

    even = time_rows % devices == 0 and space_rows % devices == 0
    if even:
        rows = time_rows // devices
        tall = round_up(rows, 16)
        offsets = row_offsets(bits[1:])
        block = (len(offsets), steps, tall, time_width)
        kept, sent = on_device(
            functools.partial(time_sum_body, offsets, rows),
            (packed, before, after),
            [shape(block, F32), shape(block, BF16)],
            [pltpu.VMEM((round_up(time_rows + tall, 8), time_width), F32)],
        )
        came = swap(sent, "row", 1)
        for bit in bits[1:]:
            block = (block[0] // 2, *block[1:])
            kept, sent = on_device(fold_body, (kept, came), [shape(block, F32), shape(block, BF16)])
            came = swap(sent, "row", bit)

        rows = space_rows // devices
        period, layout = segments(width)
        deep = round_up(tall + round_up(-(-rows // period), 8) * len(layout), 16)
        piece = (deep, LANES)
        scratch = (round_up(space_rows + 8 * period + rows, 8), LANES)
        mine, *sends = on_device(
            functools.partial(space_sum_body, groups, rows),
            (*gathered, kept, came),
            [shape(piece, F32)] + [shape(piece, BF16)] * (steps - 1),
            [pltpu.VMEM((peers, 2 * ch, 2 * cols), BF16)] + [pltpu.VMEM(scratch, F32)] * 2,
        )
        arrived = [swap(sends[k - 1], "tm", k) for k in range(1, steps)]
        full = -(-rows // period) * len(layout)
        space_share, time_share = on_device(
            functools.partial(final_body, factor, tall, period, len(layout)),
            (mine, *arrived),
            [shape((full, LANES), F32), shape((time_rows // devices, time_width), F32)],
        )
        space_share = space_share.reshape(-1)[: rows * width]
        time_share = time_share.reshape(-1)
    else:
        total = on_device(
            time_sum_whole_body, (packed, before, after), [shape((time_rows, time_width), F32)]
        )[0]
        time_share = factor * lax.psum_scatter(
            total.reshape(-1), ("tm", "row"), scatter_dimension=0, tiled=True
        )
        total = on_device(
            functools.partial(space_sum_whole_body, groups),
            gathered,
            [shape((space_rows, width), F32)],
            [pltpu.VMEM((peers, 2 * ch, 2 * cols), BF16)],
        )[0]
        total = total.reshape(steps, peers, -1)
        total = lax.dynamic_index_in_dim(total, lax.axis_index("row"), 1, keepdims=False)
        space_share = factor * lax.psum_scatter(
            total.reshape(-1), "tm", scatter_dimension=0, tiled=True
        )

    x1, g2 = on_device(
        space_body,
        (*gathered, y1, c2, x2, weight_space),
        [shape(y1.shape, BF16), shape(y1.shape, BF16)],
        [pltpu.VMEM((peers + 2, 2 * ch, 2 * cols), BF16)],
    )
    return x1, x2, g1, g2, space_share, time_share


def solution(mesh):
    video = P("tm", "row", None, None)
    share = P(("tm", "row"))
    return jax.shard_map(
        per_device,
        mesh=mesh,
        in_specs=(video,) * 4 + (P(), P()),
        out_specs=(video,) * 4 + (share, share),
        check_vma=False,
    )
```

```python
import functools
import math

import jax
import jax.numpy as jnp
from jax import lax
from jax.experimental import pallas as pl
from jax.experimental.pallas import tpu as pltpu
from jax.sharding import PartitionSpec as P

HAAR = 0.7071067811865476
LANES = 128
F32 = jnp.float32
BF16 = jnp.bfloat16


def round_up(value, unit):
    return (value + unit - 1) // unit * unit


def on_device(body, args, outs, scratch=(), far=0):
    whole = pl.BlockSpec(memory_space=pltpu.VMEM)
    moved = sum(math.prod(a.shape) * a.dtype.itemsize for a in (*args, *outs))
    scratch = [*scratch, *(pltpu.VMEM(a.shape, a.dtype) for a in args[:far])]
    if far:
        scratch.append(pltpu.SemaphoreType.DMA((far,)))
    return pl.pallas_call(
        body,
        out_shape=outs,
        in_specs=[pl.BlockSpec(memory_space=pltpu.HBM)] * far + [whole] * (len(args) - far),
        out_specs=[whole] * len(outs),
        scratch_shapes=scratch,
        compiler_params=pltpu.CompilerParams(vmem_limit_bytes=40 * 1024 * 1024),
        cost_estimate=pl.CostEstimate(flops=0, bytes_accessed=moved, transcendentals=0),
    )(*[pltpu.with_memory_space_constraint(a, pltpu.HBM) for a in args[:far]], *args[far:])


def shape(dims, dtype):
    return jax.ShapeDtypeStruct(tuple(dims), dtype)


def sigmoid(v):
    return 1.0 / (1.0 + jnp.exp(-v))


def silu_slope(v):
    s = sigmoid(v)
    return s * (1.0 + v * (1.0 - s))


def dot(left, right, left_dim, right_dim):
    return lax.dot_general(
        left, right, (((left_dim,), (right_dim,)), ((), ())), preferred_element_type=F32
    )


def squeezed(ref):
    even, odd = ref[0, 0].astype(F32), ref[1, 0].astype(F32)
    return jnp.concatenate([(even + odd) * HAAR, (even - odd) * HAAR], axis=-1)


def unsqueezed(packed):
    half = packed.shape[-1] // 2
    low, high = packed[:, :half], packed[:, half:]
    return (low + high) * HAAR, (low - high) * HAAR


def fetch(far, near, sems):
    copies = [pltpu.make_async_copy(f, n, sems.at[i]) for i, (f, n) in enumerate(zip(far, near))]
    for copy in copies:
        copy.start()
    for copy in copies:
        copy.wait()


def open_body(y_far, cot_far, out_ref, y_ref, cot_ref, sems):
    fetch((y_far, cot_far), (y_ref, cot_ref), sems)
    sq = squeezed(y_ref)
    cols = sq.shape[0]
    out_ref[:cols] = (sq * sigmoid(sq)).astype(BF16)
    out_ref[cols:] = squeezed(cot_ref).astype(BF16)


def centre_body(y1_far, y2_far, c1_far, weight_far, own, *refs):
    (forth, back, slope, base, weight_out), (y1, y2, c1, weight, sems) = refs[:5], refs[5:]
    fetch((y1_far, y2_far, c1_far, weight_far), (y1, y2, c1, weight), sems)
    cols = own.shape[0] // 2
    groups, width = weight.shape[1:3]
    for q in range(groups):
        lanes = slice(q * width, (q + 1) * width)
        forth[:, lanes] = dot(own[:cols, lanes], weight[1, q], 1, 0)
        back[:, lanes] = dot(own[cols:, lanes], weight[1, q], 1, 1)
    slope[...] = silu_slope(squeezed(y1))
    for f in range(2):
        base[0, f] = y2[f, 0]
        base[1, f] = c1[f, 0]
    weight_out[...] = weight[...]


def time_body(before, after, forth0, back0, slope, base, weight, x2_out, g1_out, act_out, cot_out):
    cols = forth0.shape[0]
    groups, width = weight.shape[1:3]
    forth, back = [], []
    for q in range(groups):
        lanes = slice(q * width, (q + 1) * width)
        forth.append(
            dot(before[:cols, lanes], weight[0, q], 1, 0)
            + forth0[:, lanes]
            + dot(after[:cols, lanes], weight[2, q], 1, 0)
        )
        back.append(
            dot(after[cols:, lanes], weight[0, q], 1, 1)
            + back0[:, lanes]
            + dot(before[cols:, lanes], weight[2, q], 1, 1)
        )
    branch = unsqueezed(jnp.concatenate(forth, axis=-1))
    back = unsqueezed(jnp.concatenate(back, axis=-1) * slope[...])
    acts, cots = [], []
    for f in range(2):
        x2 = (base[0, f].astype(F32) - branch[f].astype(BF16).astype(F32)).astype(BF16)
        g1 = (base[1, f].astype(F32) + back[f].astype(BF16).astype(F32)).astype(BF16)
        x2_out[f, 0] = x2
        g1_out[f, 0] = g1
        v = x2.astype(F32)
        acts.append(v * sigmoid(v))
        cots.append(g1.astype(F32))
    act_out[...] = jnp.concatenate(acts, axis=0).T.astype(BF16)
    cot_out[...] = jnp.concatenate(cots, axis=0).T.astype(BF16)


def time_terms(owns, afters, total):
    cols = owns[0].shape[0] // 2
    width = total.shape[1]
    groups = owns[0].shape[1] // width
    acts, cots = [], []
    for refs in (owns, afters):
        act = jnp.concatenate([ref[:cols] for ref in refs], axis=0)
        acts.append(act.astype(F32).T.astype(BF16))
        cots.append(jnp.concatenate([ref[cols:] for ref in refs], axis=0))
    for k, (act, cot) in enumerate(((acts[0], cots[1]), (acts[0], cots[0]), (acts[1], cots[0]))):
        for q in range(groups):
            part = slice(q * width, (q + 1) * width)
            term = dot(act[part], cot[:, part], 1, 0)
            total[pl.ds((k * groups + q) * width, width), :] = term


def time_sum_body(rows, *refs):
    (keep, send, total), refs = refs[-3:], refs[:-3]
    time_terms(refs[0::2], refs[1::2], total)
    me, peers, steps = lax.axis_index("row"), lax.axis_size("row"), lax.axis_size("tm")
    held = keep.shape[1]
    for t in range(steps):
        keep[t] = total[pl.ds((t * peers + me) * rows, held), :]
        send[t] = total[pl.ds((t * peers + (me ^ 1)) * rows, held), :].astype(BF16)


def time_sum_whole_body(own, after, total):
    time_terms((own,), (after,), total)


def space_terms(slots, rows_ref, cols, store):
    peers = len(slots) // 2
    me = lax.axis_index("row")
    ch = rows_ref.shape[1] // 2
    for k in range(peers):
        rows_ref[me ^ k, :ch] = slots[2 * k][...]
        rows_ref[me ^ k, ch:] = slots[2 * k + 1][...]
    column = lax.broadcasted_iota(jnp.int32, (ch, LANES), 1) % cols
    act, shifts = [], ([], [], [])
    for r in range(peers):
        act.append(rows_ref[r, :ch])
        cot = rows_ref[r, ch:]
        wide = cot.astype(F32)
        later = jnp.where(column == cols - 1, 0.0, pltpu.roll(wide, LANES - 1, 1))
        sooner = jnp.where(column == 0, 0.0, pltpu.roll(wide, 1, 1))
        for held, value in zip(shifts, (later.astype(BF16), cot, sooner.astype(BF16))):
            held.append(value)
    for a in range(3):
        pairs = [(r, r - a + 1) for r in range(peers) if 0 <= r - a + 1 < peers]
        left = jnp.concatenate([act[r] for r, _ in pairs], axis=1)
        for b in range(3):
            right = jnp.concatenate([shifts[b][r] for _, r in pairs], axis=1)
            store(a * 3 + b, left, right)


def segments(width):
    period = LANES // math.gcd(width, LANES)
    found = []
    for j in range(period * width // LANES):
        row, lane = [], 0
        while lane < LANES:
            at = j * LANES + lane
            source, column = divmod(at, width)
            tile, first = divmod(column, LANES)
            row.append((lane, source, tile, (lane - first) % LANES))
            lane += min(LANES - first, width - column, LANES - lane)
        found.append(row)
    return period, found


def space_sum_body(groups, rows, *refs):
    peers, steps = lax.axis_size("row"), lax.axis_size("tm")
    slots, (kept, came), refs = refs[: 2 * peers], refs[2 * peers : 2 * peers + 2], refs[2 * peers + 2 :]
    mine, sends, (rows_ref, main, rest) = refs[0], refs[1:steps], refs[steps:]
    ch = rows_ref.shape[1] // 2
    width = ch // groups

    def store(tap, left, right):
        for q in range(groups):
            part = slice(q * width, (q + 1) * width)
            term = dot(left[part], right[part], 1, 1)
            at = pl.ds((tap * groups + q) * width, width)
            main[at, :] = term[:, :LANES]
            rest[at, : width - LANES] = term[:, LANES:]

    space_terms(slots, rows_ref, LANES // 2, store)
    period, layout = segments(width)
    held = round_up(-(-rows // period), 8)
    lane = lax.broadcasted_iota(jnp.int32, (held, LANES), 1)
    here, me = lax.axis_index("tm"), lax.axis_index("row")
    early = kept.shape[1]
    for k in range(steps):
        t = here ^ k
        start = (t * peers + me) * rows
        rolled = {}

        def source(j, tile, amount):
            if (j, tile, amount) not in rolled:
                ref = (main, rest)[tile]
                value = ref[pl.ds(start + j, held, stride=period), :]
                rolled[j, tile, amount] = pltpu.roll(value, amount, 1) if amount else value
            return rolled[j, tile, amount]

        parts = [kept[t] + came[t].astype(F32)]
        for row in layout:
            value = None
            for first, j, tile, amount in row:
                piece = source(j, tile, amount)
                value = piece if value is None else jnp.where(lane < first, value, piece)
            parts.append(value)
        blank = mine.shape[0] - early - held * len(layout)
        if blank:
            parts.append(jnp.zeros((blank, LANES), F32))
        piece = jnp.concatenate(parts, axis=0)
        if k == 0:
            mine[...] = piece
        else:
            sends[k - 1][...] = piece.astype(BF16)


def space_sum_whole_body(groups, *refs):
    peers = lax.axis_size("row")
    slots, (total, rows_ref) = refs[: 2 * peers], refs[2 * peers :]
    ch = rows_ref.shape[1] // 2
    width = ch // groups

    def store(tap, left, right):
        for q in range(groups):
            part = slice(q * width, (q + 1) * width)
            at = pl.ds((tap * groups + q) * width, width)
            total[at, :] = dot(left[part], right[part], 1, 1)

    space_terms(slots, rows_ref, LANES // 2, store)


def final_body(factor, early, period, stride, *refs):
    (mine, *came), (space_out, time_out) = refs[:-2], refs[-2:]
    total = mine[...]
    for ref in came:
        total = total + ref[...].astype(F32)
    total = total * factor
    time_out[...] = total[: time_out.shape[0]]
    held = space_out.shape[0] // stride
    tall = (total.shape[0] - early) // stride // 8 * 8
    for j in range(stride):
        first = early + j * tall
        space_out[pl.ds(j, held, stride=stride), :] = total[first : first + held]


def space_body(*refs):
    peers = lax.axis_size("row")
    slots, refs = refs[: 2 * peers], refs[2 * peers :]
    y1, c2, x2, g1, weight, x1_out, x2_out, g1_out, g2_out, rows_ref = refs
    x2_out[...] = x2[...]
    g1_out[...] = g1[...]
    me = lax.axis_index("row")
    cols, ch = y1.shape[2:]
    groups, width = weight.shape[2:4]
    rows_ref[0] = jnp.zeros(rows_ref.shape[1:], BF16)
    rows_ref[peers + 1] = jnp.zeros(rows_ref.shape[1:], BF16)
    for k in range(peers):
        rows_ref[(me ^ k) + 1, :ch] = slots[2 * k][...]
        rows_ref[(me ^ k) + 1, ch:] = slots[2 * k + 1][...]
    column = lax.broadcasted_iota(jnp.int32, (LANES, width), 0) % cols
    forth, back = [None] * groups, [None] * groups
    for a in range(3):
        row = rows_ref[me + a].astype(F32).T
        for q in range(groups):
            for first, sums in ((0, forth), (ch, back)):
                value = row[:, first + q * width : first + (q + 1) * width]
                sooner = jnp.where(column == 0, 0.0, pltpu.roll(value, 1, 0))
                later = jnp.where(column == cols - 1, 0.0, pltpu.roll(value, LANES - 1, 0))
                for b, moved in enumerate((sooner, value, later)):
                    if first:
                        term = dot(moved.astype(BF16), weight[2 - a, 2 - b, q], 1, 1)
                    else:
                        term = dot(moved.astype(BF16), weight[a, b, q], 1, 0)
                    sums[q] = term if sums[q] is None else sums[q] + term
    forth = jnp.concatenate(forth, axis=-1)
    back = jnp.concatenate(back, axis=-1)
    for f in range(2):
        part = slice(f * cols, (f + 1) * cols)
        x1_out[f, 0] = (y1[f, 0].astype(F32) - forth[part]).astype(BF16)
        slope = silu_slope(x2[f, 0].astype(F32))
        g2_out[f, 0] = (c2[f, 0].astype(F32) + slope * back[part]).astype(BF16)


def swap(x, axis, bit):
    return lax.ppermute(x, axis, [(i, i ^ bit) for i in range(lax.axis_size(axis))])


def gather(x, axis, bits):
    slots = {0: x}
    for bit in reversed(bits):
        for k in list(slots):
            slots[k ^ bit] = swap(slots[k], axis, bit)
    return [slots[k] for k in sorted(slots)]


def per_device(y1, y2, c1, c2, weight_space, temporal_weight):
    steps, peers = lax.axis_size("tm"), lax.axis_size("row")
    devices = steps * peers
    frames, rows_here, cols, ch = y1.shape
    groups = weight_space.shape[2]
    width = ch // groups
    taps = weight_space.shape[0] * weight_space.shape[1]
    factor = 1.0 / math.sqrt(frames * rows_here * cols * devices)
    time_groups, time_width = temporal_weight.shape[1:3]
    time_rows = 3 * time_groups * time_width
    space_rows = taps * ch

    packed = on_device(open_body, (y1, c2), [shape((2 * cols, 2 * ch), BF16)], far=2)[0]
    up = [(i, i + 1) for i in range(steps - 1)]
    after = lax.ppermute(packed, "tm", [(i + 1, i) for i in range(steps - 1)])
    before = lax.ppermute(packed, "tm", [(i, i + 1) for i in range(steps - 1)])
    wide = shape((cols, 2 * ch), F32)
    centre = on_device(
        centre_body,
        (y1, y2, c1, temporal_weight, packed),
        [wide] * 3 + [shape((2, 2, cols, ch), BF16), shape(temporal_weight.shape, BF16)],
        far=4,
    )

    even = time_rows % devices == 0 and space_rows % devices == 0
    bits = [1 << i for i in range(peers.bit_length() - 1)]
    if even:
        rows = time_rows // devices
        tall = round_up(rows, 16)
        part = (steps, tall, time_width)
        held, centre = lax.optimization_barrier((after, centre))
        owns, afters = gather(packed, "row", bits[1:]), gather(held, "row", bits[1:])
        kept, sent = on_device(
            functools.partial(time_sum_body, rows),
            [v for pair in zip(owns, afters) for v in pair],
            [shape(part, F32), shape(part, BF16)],
            [pltpu.VMEM((round_up(time_rows + tall, 8), time_width), F32)],
        )
        came = swap(sent, "row", 1)

    x2, g1, act, cot = on_device(
        time_body,
        (before, after, *centre),
        [shape(y1.shape, BF16)] * 2 + [shape((ch, 2 * cols), BF16)] * 2,
    )
    pairs = zip(gather(act, "row", bits), gather(cot, "row", bits))
    gathered = [v for pair in pairs for v in pair]

    if even:
        rows = space_rows // devices
        period, layout = segments(width)
        deep = round_up(tall + round_up(-(-rows // period), 8) * len(layout), 16)
        piece = (deep, LANES)
        scratch = (round_up(space_rows + 8 * period + rows, 8), LANES)
        mine, *sends = on_device(
            functools.partial(space_sum_body, groups, rows),
            (*gathered, kept, came),
            [shape(piece, F32)] + [shape(piece, BF16)] * (steps - 1),
            [pltpu.VMEM((peers, 2 * ch, 2 * cols), BF16)] + [pltpu.VMEM(scratch, F32)] * 2,
        )
        arrived = [swap(sends[k - 1], "tm", k) for k in range(1, steps)]
        full = -(-rows // period) * len(layout)
        space_share, time_share = on_device(
            functools.partial(final_body, factor, tall, period, len(layout)),
            (mine, *arrived),
            [shape((full, LANES), F32), shape((time_rows // devices, time_width), F32)],
        )
        space_share = space_share.reshape(-1)[: rows * width]
        time_share = time_share.reshape(-1)
    else:
        total = on_device(
            time_sum_whole_body, (packed, after), [shape((time_rows, time_width), F32)]
        )[0]
        time_share = factor * lax.psum_scatter(
            total.reshape(-1), ("tm", "row"), scatter_dimension=0, tiled=True
        )
        total = on_device(
            functools.partial(space_sum_whole_body, groups),
            gathered,
            [shape((space_rows, width), F32)],
            [pltpu.VMEM((peers, 2 * ch, 2 * cols), BF16)],
        )[0]
        total = total.reshape(steps, peers, -1)
        total = lax.dynamic_index_in_dim(total, lax.axis_index("row"), 1, keepdims=False)
        space_share = factor * lax.psum_scatter(
            total.reshape(-1), "tm", scatter_dimension=0, tiled=True
        )

    x1, x2, g1, g2 = on_device(
        space_body,
        (*gathered, y1, c2, x2, g1, weight_space),
        [shape(y1.shape, BF16)] * 4,
        [pltpu.VMEM((peers + 2, 2 * ch, 2 * cols), BF16)],
    )
    return x1, x2, g1, g2, space_share, time_share


def solution(mesh):
    video = P("tm", "row", None, None)
    share = P(("tm", "row"))
    return jax.shard_map(
        per_device,
        mesh=mesh,
        in_specs=(video,) * 4 + (P(), P()),
        out_specs=(video,) * 4 + (share, share),
        check_vma=False,
    )
```

```python
import functools
import math

import jax
import jax.numpy as jnp
from jax import lax
from jax.experimental import pallas as pl
from jax.experimental.pallas import tpu as pltpu
from jax.sharding import PartitionSpec as P

HAAR = 0.7071067811865476
LANES = 128
F32 = jnp.float32
BF16 = jnp.bfloat16


def round_up(value, unit):
    return (value + unit - 1) // unit * unit


def on_device(body, args, outs, scratch=(), far=0):
    whole = pl.BlockSpec(memory_space=pltpu.VMEM)
    moved = sum(math.prod(a.shape) * a.dtype.itemsize for a in (*args, *outs))
    scratch = [*scratch, *(pltpu.VMEM(a.shape, a.dtype) for a in args[:far])]
    if far:
        scratch.append(pltpu.SemaphoreType.DMA((far,)))
    return pl.pallas_call(
        body,
        out_shape=outs,
        in_specs=[pl.BlockSpec(memory_space=pltpu.HBM)] * far + [whole] * (len(args) - far),
        out_specs=[whole] * len(outs),
        scratch_shapes=scratch,
        compiler_params=pltpu.CompilerParams(vmem_limit_bytes=40 * 1024 * 1024),
        cost_estimate=pl.CostEstimate(flops=0, bytes_accessed=moved, transcendentals=0),
    )(*[pltpu.with_memory_space_constraint(a, pltpu.HBM) for a in args[:far]], *args[far:])


def shape(dims, dtype):
    return jax.ShapeDtypeStruct(tuple(dims), dtype)


def sigmoid(v):
    return 1.0 / (1.0 + jnp.exp(-v))


def silu_slope(v):
    s = sigmoid(v)
    return s * (1.0 + v * (1.0 - s))


def dot(left, right, left_dim, right_dim):
    return lax.dot_general(
        left, right, (((left_dim,), (right_dim,)), ((), ())), preferred_element_type=F32
    )


def squeezed(ref):
    even, odd = ref[0, 0].astype(F32), ref[1, 0].astype(F32)
    return jnp.concatenate([(even + odd) * HAAR, (even - odd) * HAAR], axis=-1)


def unsqueezed(packed):
    half = packed.shape[-1] // 2
    low, high = packed[:, :half], packed[:, half:]
    return (low + high) * HAAR, (low - high) * HAAR


def fetch(far, near, sems):
    copies = [pltpu.make_async_copy(f, n, sems.at[i]) for i, (f, n) in enumerate(zip(far, near))]
    for copy in copies:
        copy.start()
    for copy in copies:
        copy.wait()


def open_body(y_far, cot_far, out_ref, y_ref, cot_ref, sems):
    fetch((y_far, cot_far), (y_ref, cot_ref), sems)
    sq = squeezed(y_ref)
    cols = sq.shape[0]
    out_ref[:cols] = (sq * sigmoid(sq)).astype(BF16)
    out_ref[cols:] = squeezed(cot_ref).astype(BF16)


def centre_body(y1_far, y2_far, c1_far, weight_far, own, *refs):
    (forth, back, slope, base, weight_out), (y1, y2, c1, weight, sems) = refs[:5], refs[5:]
    fetch((y1_far, y2_far, c1_far, weight_far), (y1, y2, c1, weight), sems)
    cols = own.shape[0] // 2
    groups, width = weight.shape[1:3]
    for q in range(groups):
        lanes = slice(q * width, (q + 1) * width)
        forth[:, lanes] = dot(own[:cols, lanes], weight[1, q], 1, 0)
        back[:, lanes] = dot(own[cols:, lanes], weight[1, q], 1, 1)
    slope[...] = silu_slope(squeezed(y1))
    for f in range(2):
        base[0, f] = y2[f, 0]
        base[1, f] = c1[f, 0]
    weight_out[...] = weight[...]


def time_body(before, after, forth0, back0, slope, base, weight, x2_out, g1_out, act_out, cot_out):
    cols = forth0.shape[0]
    groups, width = weight.shape[1:3]
    forth, back = [], []
    for q in range(groups):
        lanes = slice(q * width, (q + 1) * width)
        forth.append(
            dot(before[:cols, lanes], weight[0, q], 1, 0)
            + forth0[:, lanes]
            + dot(after[:cols, lanes], weight[2, q], 1, 0)
        )
        back.append(
            dot(after[cols:, lanes], weight[0, q], 1, 1)
            + back0[:, lanes]
            + dot(before[cols:, lanes], weight[2, q], 1, 1)
        )
    branch = unsqueezed(jnp.concatenate(forth, axis=-1))
    back = unsqueezed(jnp.concatenate(back, axis=-1) * slope[...])
    acts, cots = [], []
    for f in range(2):
        x2 = (base[0, f].astype(F32) - branch[f].astype(BF16).astype(F32)).astype(BF16)
        g1 = (base[1, f].astype(F32) + back[f].astype(BF16).astype(F32)).astype(BF16)
        x2_out[f, 0] = x2
        g1_out[f, 0] = g1
        v = x2.astype(F32)
        acts.append(v * sigmoid(v))
        cots.append(g1.astype(F32))
    act_out[...] = jnp.concatenate(acts, axis=0).T.astype(BF16)
    cot_out[...] = jnp.concatenate(cots, axis=0).T.astype(BF16)


def time_terms(owns, afters, total):
    cols = owns[0].shape[0] // 2
    width = total.shape[1]
    groups = owns[0].shape[1] // width
    acts, cots = [], []
    for refs in (owns, afters):
        act = jnp.concatenate([ref[:cols] for ref in refs], axis=0)
        acts.append(act.astype(F32).T.astype(BF16))
        cots.append(jnp.concatenate([ref[cols:] for ref in refs], axis=0))
    for k, (act, cot) in enumerate(((acts[0], cots[1]), (acts[0], cots[0]), (acts[1], cots[0]))):
        for q in range(groups):
            part = slice(q * width, (q + 1) * width)
            term = dot(act[part], cot[:, part], 1, 0)
            total[pl.ds((k * groups + q) * width, width), :] = term


def time_sum_body(rows, *refs):
    (keep, send, total), refs = refs[-3:], refs[:-3]
    time_terms(refs[0::2], refs[1::2], total)
    me, peers, steps = lax.axis_index("row"), lax.axis_size("row"), lax.axis_size("tm")
    held = keep.shape[1]
    for t in range(steps):
        keep[t] = total[pl.ds((t * peers + me) * rows, held), :]
        send[t] = total[pl.ds((t * peers + (me ^ 1)) * rows, held), :].astype(BF16)


def time_sum_whole_body(own, after, total):
    time_terms((own,), (after,), total)


def space_terms(slots, rows_ref, cols, store):
    peers = len(slots) // 2
    me = lax.axis_index("row")
    ch = rows_ref.shape[1] // 2
    for k in range(peers):
        rows_ref[me ^ k, :ch] = slots[2 * k][...]
        rows_ref[me ^ k, ch:] = slots[2 * k + 1][...]
    column = lax.broadcasted_iota(jnp.int32, (ch, LANES), 1) % cols
    act, shifts = [], ([], [], [])
    for r in range(peers):
        act.append(rows_ref[r, :ch])
        cot = rows_ref[r, ch:]
        wide = cot.astype(F32)
        later = jnp.where(column == cols - 1, 0.0, pltpu.roll(wide, LANES - 1, 1))
        sooner = jnp.where(column == 0, 0.0, pltpu.roll(wide, 1, 1))
        for held, value in zip(shifts, (later.astype(BF16), cot, sooner.astype(BF16))):
            held.append(value)
    for a in range(3):
        pairs = [(r, r - a + 1) for r in range(peers) if 0 <= r - a + 1 < peers]
        left = jnp.concatenate([act[r] for r, _ in pairs], axis=1)
        for b in range(3):
            right = jnp.concatenate([shifts[b][r] for _, r in pairs], axis=1)
            store(a * 3 + b, left, right)


def segments(width):
    period = LANES // math.gcd(width, LANES)
    found = []
    for j in range(period * width // LANES):
        row, lane = [], 0
        while lane < LANES:
            at = j * LANES + lane
            source, column = divmod(at, width)
            tile, first = divmod(column, LANES)
            row.append((lane, source, tile, (lane - first) % LANES))
            lane += min(LANES - first, width - column, LANES - lane)
        found.append(row)
    return period, found


def space_sum_body(groups, rows, time_rows, *refs):
    peers, steps = lax.axis_size("row"), lax.axis_size("tm")
    slots, (kept, came), refs = refs[: 2 * peers], refs[2 * peers : 2 * peers + 2], refs[2 * peers + 2 :]
    mine, sends, (rows_ref, main, rest) = refs[0], refs[1:steps], refs[steps:]
    ch = rows_ref.shape[1] // 2
    width = ch // groups

    def store(tap, left, right):
        for q in range(groups):
            part = slice(q * width, (q + 1) * width)
            term = dot(left[part], right[part], 1, 1)
            at = pl.ds((tap * groups + q) * width, width)
            main[at, :] = term[:, :LANES]
            rest[at, : width - LANES] = term[:, LANES:]

    space_terms(slots, rows_ref, LANES // 2, store)
    period, layout = segments(width)
    held = round_up(-(-rows // period), 8)
    lane = lax.broadcasted_iota(jnp.int32, (held, LANES), 1)
    here, me = lax.axis_index("tm"), lax.axis_index("row")
    short = -(-rows // period)
    for k in range(steps):
        t = here ^ k
        start = (t * peers + me) * rows
        rolled = {}

        def source(j, tile, amount):
            if (j, tile, amount) not in rolled:
                ref = (main, rest)[tile]
                value = ref[pl.ds(start + j, held, stride=period), :]
                rolled[j, tile, amount] = pltpu.roll(value, amount, 1) if amount else value
            return rolled[j, tile, amount]

        parts = [(kept[t] + came[t].astype(F32))[:time_rows]]
        for row in layout:
            value = None
            for first, j, tile, amount in row:
                piece = source(j, tile, amount)
                value = piece if value is None else jnp.where(lane < first, value, piece)
            parts.append(value[:short])
        blank = mine.shape[0] - time_rows - short * len(layout)
        if blank:
            parts.append(jnp.zeros((blank, LANES), F32))
        piece = jnp.concatenate(parts, axis=0)
        if k == 0:
            mine[...] = piece
        else:
            sends[k - 1][...] = piece.astype(BF16)


def space_sum_whole_body(groups, *refs):
    peers = lax.axis_size("row")
    slots, (total, rows_ref) = refs[: 2 * peers], refs[2 * peers :]
    ch = rows_ref.shape[1] // 2
    width = ch // groups

    def store(tap, left, right):
        for q in range(groups):
            part = slice(q * width, (q + 1) * width)
            at = pl.ds((tap * groups + q) * width, width)
            total[at, :] = dot(left[part], right[part], 1, 1)

    space_terms(slots, rows_ref, LANES // 2, store)


def final_body(factor, stride, *refs):
    (mine, *came), (space_out, time_out) = refs[:-2], refs[-2:]
    total = mine[...]
    for ref in came:
        total = total + ref[...].astype(F32)
    total = total * factor
    first, short = time_out.shape[0], space_out.shape[0] // stride
    time_out[...] = total[:first]
    for j in range(stride):
        space_out[pl.ds(j, short, stride=stride), :] = total[first + j * short : first + (j + 1) * short]


def space_body(*refs):
    peers = lax.axis_size("row")
    slots, refs = refs[: 2 * peers], refs[2 * peers :]
    y1, c2, x2, g1, weight, x1_out, x2_out, g1_out, g2_out, rows_ref = refs
    x2_out[...] = x2[...]
    g1_out[...] = g1[...]
    me = lax.axis_index("row")
    cols, ch = y1.shape[2:]
    groups, width = weight.shape[2:4]
    rows_ref[0] = jnp.zeros(rows_ref.shape[1:], BF16)
    rows_ref[peers + 1] = jnp.zeros(rows_ref.shape[1:], BF16)
    for k in range(peers):
        rows_ref[(me ^ k) + 1, :ch] = slots[2 * k][...]
        rows_ref[(me ^ k) + 1, ch:] = slots[2 * k + 1][...]
    column = lax.broadcasted_iota(jnp.int32, (LANES, width), 0) % cols
    forth, back = [None] * groups, [None] * groups
    for a in range(3):
        row = rows_ref[me + a].astype(F32).T
        for q in range(groups):
            for first, sums in ((0, forth), (ch, back)):
                value = row[:, first + q * width : first + (q + 1) * width]
                sooner = jnp.where(column == 0, 0.0, pltpu.roll(value, 1, 0))
                later = jnp.where(column == cols - 1, 0.0, pltpu.roll(value, LANES - 1, 0))
                for b, moved in enumerate((sooner, value, later)):
                    if first:
                        term = dot(moved.astype(BF16), weight[2 - a, 2 - b, q], 1, 1)
                    else:
                        term = dot(moved.astype(BF16), weight[a, b, q], 1, 0)
                    sums[q] = term if sums[q] is None else sums[q] + term
    forth = jnp.concatenate(forth, axis=-1)
    back = jnp.concatenate(back, axis=-1)
    for f in range(2):
        part = slice(f * cols, (f + 1) * cols)
        x1_out[f, 0] = (y1[f, 0].astype(F32) - forth[part]).astype(BF16)
        slope = silu_slope(x2[f, 0].astype(F32))
        g2_out[f, 0] = (c2[f, 0].astype(F32) + slope * back[part]).astype(BF16)


def swap(x, axis, bit):
    return lax.ppermute(x, axis, [(i, i ^ bit) for i in range(lax.axis_size(axis))])


def gather(x, axis, bits):
    slots = {0: x}
    for bit in reversed(bits):
        for k in list(slots):
            slots[k ^ bit] = swap(slots[k], axis, bit)
    return [slots[k] for k in sorted(slots)]


def per_device(y1, y2, c1, c2, weight_space, temporal_weight):
    steps, peers = lax.axis_size("tm"), lax.axis_size("row")
    devices = steps * peers
    frames, rows_here, cols, ch = y1.shape
    groups = weight_space.shape[2]
    width = ch // groups
    taps = weight_space.shape[0] * weight_space.shape[1]
    factor = 1.0 / math.sqrt(frames * rows_here * cols * devices)
    time_groups, time_width = temporal_weight.shape[1:3]
    time_rows = 3 * time_groups * time_width
    space_rows = taps * ch

    packed = on_device(open_body, (y1, c2), [shape((2 * cols, 2 * ch), BF16)], far=2)[0]
    up = [(i, i + 1) for i in range(steps - 1)]
    after = lax.ppermute(packed, "tm", [(i + 1, i) for i in range(steps - 1)])
    before = lax.ppermute(packed, "tm", [(i, i + 1) for i in range(steps - 1)])
    wide = shape((cols, 2 * ch), F32)
    centre = on_device(
        centre_body,
        (y1, y2, c1, temporal_weight, packed),
        [wide] * 3 + [shape((2, 2, cols, ch), BF16), shape(temporal_weight.shape, BF16)],
        far=4,
    )

    even = time_rows % devices == 0 and space_rows % devices == 0
    bits = [1 << i for i in range(peers.bit_length() - 1)]
    if even:
        rows = time_rows // devices
        tall = round_up(rows, 16)
        part = (steps, tall, time_width)
        held, centre = lax.optimization_barrier((after, centre))
        owns, afters = gather(packed, "row", bits[1:]), gather(held, "row", bits[1:])
        kept, sent = on_device(
            functools.partial(time_sum_body, rows),
            [v for pair in zip(owns, afters) for v in pair],
            [shape(part, F32), shape(part, BF16)],
            [pltpu.VMEM((round_up(time_rows + tall, 8), time_width), F32)],
        )
        came = swap(sent, "row", 1)

    x2, g1, act, cot = on_device(
        time_body,
        (before, after, *centre),
        [shape(y1.shape, BF16)] * 2 + [shape((ch, 2 * cols), BF16)] * 2,
    )
    pairs = zip(gather(act, "row", bits), gather(cot, "row", bits))
    gathered = [v for pair in pairs for v in pair]

    if even:
        rows = space_rows // devices
        period, layout = segments(width)
        full = -(-rows // period) * len(layout)
        deep = round_up(time_rows // devices + full, 16)
        piece = (deep, LANES)
        scratch = (round_up(space_rows + 8 * period + rows, 8), LANES)
        mine, *sends = on_device(
            functools.partial(space_sum_body, groups, rows, time_rows // devices),
            (*gathered, kept, came),
            [shape(piece, F32)] + [shape(piece, BF16)] * (steps - 1),
            [pltpu.VMEM((peers, 2 * ch, 2 * cols), BF16)] + [pltpu.VMEM(scratch, F32)] * 2,
        )
        order = sorted(range(1, steps), key=lambda k: (-k.bit_length(), k & 1, -k))
        arrived = [swap(sends[k - 1], "tm", k) for k in order]
        space_share, time_share = on_device(
            functools.partial(final_body, factor, len(layout)),
            (mine, *arrived),
            [shape((full, LANES), F32), shape((time_rows // devices, time_width), F32)],
        )
        space_share = space_share.reshape(-1)[: rows * width]
        time_share = time_share.reshape(-1)
    else:
        total = on_device(
            time_sum_whole_body, (packed, after), [shape((time_rows, time_width), F32)]
        )[0]
        time_share = factor * lax.psum_scatter(
            total.reshape(-1), ("tm", "row"), scatter_dimension=0, tiled=True
        )
        total = on_device(
            functools.partial(space_sum_whole_body, groups),
            gathered,
            [shape((space_rows, width), F32)],
            [pltpu.VMEM((peers, 2 * ch, 2 * cols), BF16)],
        )[0]
        total = total.reshape(steps, peers, -1)
        total = lax.dynamic_index_in_dim(total, lax.axis_index("row"), 1, keepdims=False)
        space_share = factor * lax.psum_scatter(
            total.reshape(-1), "tm", scatter_dimension=0, tiled=True
        )

    x1, x2, g1, g2 = on_device(
        space_body,
        (*gathered, y1, c2, x2, g1, weight_space),
        [shape(y1.shape, BF16)] * 4,
        [pltpu.VMEM((peers + 2, 2 * ch, 2 * cols), BF16)],
    )
    return x1, x2, g1, g2, space_share, time_share


def solution(mesh):
    video = P("tm", "row", None, None)
    share = P(("tm", "row"))
    return jax.shard_map(
        per_device,
        mesh=mesh,
        in_specs=(video,) * 4 + (P(), P()),
        out_specs=(video,) * 4 + (share, share),
        check_vma=False,
    )
```

```python
import functools
import math

import jax
import jax.numpy as jnp
from jax import lax
from jax.experimental import pallas as pl
from jax.experimental.pallas import tpu as pltpu
from jax.sharding import PartitionSpec as P

HAAR = 0.7071067811865476
LANES = 128
F32 = jnp.float32
BF16 = jnp.bfloat16


def round_up(value, unit):
    return (value + unit - 1) // unit * unit


def on_device(body, args, outs, scratch=(), far=0):
    whole = pl.BlockSpec(memory_space=pltpu.VMEM)
    moved = sum(math.prod(a.shape) * a.dtype.itemsize for a in (*args, *outs))
    scratch = [*scratch, *(pltpu.VMEM(a.shape, a.dtype) for a in args[:far])]
    if far:
        scratch.append(pltpu.SemaphoreType.DMA((far,)))
    return pl.pallas_call(
        body,
        out_shape=outs,
        in_specs=[pl.BlockSpec(memory_space=pltpu.HBM)] * far + [whole] * (len(args) - far),
        out_specs=[whole] * len(outs),
        scratch_shapes=scratch,
        compiler_params=pltpu.CompilerParams(vmem_limit_bytes=40 * 1024 * 1024),
        cost_estimate=pl.CostEstimate(flops=0, bytes_accessed=moved, transcendentals=0),
    )(*[pltpu.with_memory_space_constraint(a, pltpu.HBM) for a in args[:far]], *args[far:])


def shape(dims, dtype):
    return jax.ShapeDtypeStruct(tuple(dims), dtype)


def sigmoid(v):
    return 1.0 / (1.0 + jnp.exp(-v))


def silu_slope(v):
    s = sigmoid(v)
    return s * (1.0 + v * (1.0 - s))


def dot(left, right, left_dim, right_dim):
    return lax.dot_general(
        left, right, (((left_dim,), (right_dim,)), ((), ())), preferred_element_type=F32
    )


def squeezed(ref):
    even, odd = ref[0, 0].astype(F32), ref[1, 0].astype(F32)
    return jnp.concatenate([(even + odd) * HAAR, (even - odd) * HAAR], axis=-1)


def unsqueezed(packed):
    half = packed.shape[-1] // 2
    low, high = packed[:, :half], packed[:, half:]
    return (low + high) * HAAR, (low - high) * HAAR


def fetch(far, near, sems):
    copies = [pltpu.make_async_copy(f, n, sems.at[i]) for i, (f, n) in enumerate(zip(far, near))]
    for copy in copies:
        copy.start()
    for copy in copies:
        copy.wait()


def open_body(y_far, cot_far, out_ref, y_ref, cot_ref, sems):
    fetch((y_far, cot_far), (y_ref, cot_ref), sems)
    sq = squeezed(y_ref)
    cols = sq.shape[0]
    out_ref[:cols] = (sq * sigmoid(sq)).astype(BF16)
    out_ref[cols:] = squeezed(cot_ref).astype(BF16)


def centre_body(y1_far, y2_far, c1_far, weight_far, own, *refs):
    (forth, back, slope, base, weight_out), (y1, y2, c1, weight, sems) = refs[:5], refs[5:]
    fetch((y1_far, y2_far, c1_far, weight_far), (y1, y2, c1, weight), sems)
    cols = own.shape[0] // 2
    groups, width = weight.shape[1:3]
    for q in range(groups):
        lanes = slice(q * width, (q + 1) * width)
        forth[:, lanes] = dot(own[:cols, lanes], weight[1, q], 1, 0)
        back[:, lanes] = dot(own[cols:, lanes], weight[1, q], 1, 1)
    slope[...] = silu_slope(squeezed(y1))
    for f in range(2):
        base[0, f] = y2[f, 0]
        base[1, f] = c1[f, 0]
    weight_out[...] = weight[...]


def time_body(near, far, forth0, back0, slope, base, weight, x2_out, g1_out, held_out):
    cols = forth0.shape[0]
    groups, width = weight.shape[1:3]
    tap = jnp.where(lax.axis_index("tm") % 2 == 0, 2, 0)
    forth, back = [], []
    for q in range(groups):
        lanes = slice(q * width, (q + 1) * width)
        forth.append(
            forth0[:, lanes]
            + dot(near[:cols, lanes], weight[tap, q], 1, 0)
            + dot(far[:cols, lanes], weight[2 - tap, q], 1, 0)
        )
        back.append(
            back0[:, lanes]
            + dot(near[cols:, lanes], weight[2 - tap, q], 1, 1)
            + dot(far[cols:, lanes], weight[tap, q], 1, 1)
        )
    branch = unsqueezed(jnp.concatenate(forth, axis=-1))
    back = unsqueezed(jnp.concatenate(back, axis=-1) * slope[...])
    acts, cots = [], []
    for f in range(2):
        x2 = (base[0, f].astype(F32) - branch[f].astype(BF16).astype(F32)).astype(BF16)
        g1 = (base[1, f].astype(F32) + back[f].astype(BF16).astype(F32)).astype(BF16)
        x2_out[f, 0] = x2
        g1_out[f, 0] = g1
        v = x2.astype(F32)
        acts.append(v * sigmoid(v))
        cots.append(g1.astype(F32))
    ch = held_out.shape[0] // 2
    held_out[:ch] = jnp.concatenate(acts, axis=0).T.astype(BF16)
    held_out[ch:] = jnp.concatenate(cots, axis=0).T.astype(BF16)


def time_terms(own, pairs, total):
    cols = own.shape[0] // 2
    width = total.shape[1]
    groups = own.shape[1] // width
    act = own[:cols].astype(F32).T.astype(BF16)
    for k, cot in pairs:
        for q in range(groups):
            part = slice(q * width, (q + 1) * width)
            at = pl.multiple_of((k * groups + q) * width, width)
            total[pl.ds(at, width), :] = dot(act[part], cot[cols:, part], 1, 0)


def near_tap():
    return jnp.where(lax.axis_index("tm") % 2 == 0, 0, 2)


def time_near_body(own, near, total):
    total[...] = jnp.zeros_like(total)
    time_terms(own, ((1, own), (near_tap(), near)), total)


def time_sum_body(offsets, rows, own, far, early, keep, *refs):
    sends, total = refs[:-1], refs[-1]
    total[: early.shape[0]] = early[...]
    time_terms(own, ((2 - near_tap(), far),), total)
    me, peers, steps = lax.axis_index("row"), lax.axis_size("row"), lax.axis_size("tm")
    held, size = keep.shape[2], sends[0].shape[0]
    for u, offset in enumerate(offsets):
        for t in range(steps):
            mine = (t * peers + (me ^ offset)) * rows
            other = (t * peers + (me ^ offset ^ 1)) * rows
            keep[u, t] = total[pl.ds(mine, held), :]
            part = sends[(u * steps + t) // size]
            part[t % size] = total[pl.ds(other, held), :].astype(BF16)


def time_sum_whole_body(own, far, early, total):
    total[...] = early[...]
    time_terms(own, ((2 - near_tap(), far),), total)


def fold_body(kept, *refs):
    *came, keep, send = refs
    steps, size = kept.shape[1], came[0].shape[0]
    half = keep.shape[0]
    for i, ref in enumerate(came):
        u, t = divmod(i * size, steps)
        total = kept[u, t : t + size] + ref[...].astype(F32)
        if u < half:
            keep[u, t : t + size] = total
        else:
            send[u - half, t : t + size] = total.astype(BF16)


def place(slots, rows_ref, lead):
    me, ch = lax.axis_index("row"), rows_ref.shape[1]
    peers = lax.axis_size("row")
    whole = peers // 2 + 1
    rest = slots[whole:]
    parts = len(rest) // (peers - whole) if rest else 1
    slots = [(v,) for v in slots[:whole]] + [
        rest[i : i + parts] for i in range(0, len(rest), parts)
    ]
    for k, refs in zip(slot_order(peers), slots):
        for j, ref in enumerate(refs):
            size = ch // len(refs)
            rows_ref[(me ^ k) + lead, j * size : (j + 1) * size] = ref[...]


def space_terms(slots, rows_ref, cols, store):
    peers = lax.axis_size("row")
    ch = rows_ref.shape[1] // 2
    place(slots, rows_ref, 0)
    column = lax.broadcasted_iota(jnp.int32, (ch, LANES), 1) % cols
    act, shifts = [], ([], [], [])
    for r in range(peers):
        act.append(rows_ref[r, :ch])
        cot = rows_ref[r, ch:]
        wide = cot.astype(F32)
        later = jnp.where(column == cols - 1, 0.0, pltpu.roll(wide, LANES - 1, 1))
        sooner = jnp.where(column == 0, 0.0, pltpu.roll(wide, 1, 1))
        for held, value in zip(shifts, (later.astype(BF16), cot, sooner.astype(BF16))):
            held.append(value)
    for a in range(3):
        pairs = [(r, r - a + 1) for r in range(peers) if 0 <= r - a + 1 < peers]
        left = jnp.concatenate([act[r] for r, _ in pairs], axis=1)
        for b in range(3):
            right = jnp.concatenate([shifts[b][r] for _, r in pairs], axis=1)
            store(a * 3 + b, left, right)


def segments(width):
    period = LANES // math.gcd(width, LANES)
    found = []
    for j in range(period * width // LANES):
        row, lane = [], 0
        while lane < LANES:
            at = j * LANES + lane
            source, column = divmod(at, width)
            tile, first = divmod(column, LANES)
            row.append((lane, source, tile, (lane - first) % LANES))
            lane += min(LANES - first, width - column, LANES - lane)
        found.append(row)
    return period, found


def space_sum_body(count, groups, rows, time_rows, *refs):
    peers, steps = lax.axis_size("row"), lax.axis_size("tm")
    slots, refs = refs[:count], refs[count:]
    out, rows_ref, main, rest = refs
    ch = rows_ref.shape[1] // 2
    width = ch // groups

    def store(tap, left, right):
        for q in range(groups):
            part = slice(q * width, (q + 1) * width)
            term = dot(left[part], right[part], 1, 1)
            at = pl.ds((tap * groups + q) * width, width)
            main[at, :] = term[:, :LANES]
            rest[at, : width - LANES] = term[:, LANES:]

    space_terms(slots, rows_ref, LANES // 2, store)
    period, layout = segments(width)
    held = round_up(-(-rows // period), 8)
    lane = lax.broadcasted_iota(jnp.int32, (held, LANES), 1)
    here, me = lax.axis_index("tm"), lax.axis_index("row")
    short = -(-rows // period)
    for k in range(steps):
        t = here ^ k
        start = (t * peers + me) * rows
        rolled = {}

        def source(j, tile, amount):
            if (j, tile, amount) not in rolled:
                ref = (main, rest)[tile]
                value = ref[pl.ds(start + j, held, stride=period), :]
                rolled[j, tile, amount] = pltpu.roll(value, amount, 1) if amount else value
            return rolled[j, tile, amount]

        parts = [jnp.zeros((time_rows, LANES), F32)]
        for row in layout:
            value = None
            for first, j, tile, amount in row:
                piece = source(j, tile, amount)
                value = piece if value is None else jnp.where(lane < first, value, piece)
            parts.append(value[:short])
        blank = out.shape[1] - time_rows - short * len(layout)
        if blank:
            parts.append(jnp.zeros((blank, LANES), F32))
        out[k] = jnp.concatenate(parts, axis=0)


def join_body(time_rows, pieces, kept, came, mine, *sends):
    tall = kept.shape[2]
    row = lax.broadcasted_iota(jnp.int32, (tall, LANES), 0)
    for k in range(pieces.shape[0]):
        t = lax.axis_index("tm") ^ k
        terms = jnp.where(row < time_rows, kept[0, t] + came[0, t].astype(F32), 0.0)
        piece = jnp.concatenate([pieces[k, :tall] + terms, pieces[k, tall:]], axis=0)
        if k == 0:
            mine[...] = piece
        else:
            sends[k - 1][...] = piece.astype(BF16)


def space_sum_whole_body(count, groups, *refs):
    slots, (total, rows_ref) = refs[:count], refs[count:]
    ch = rows_ref.shape[1] // 2
    width = ch // groups

    def store(tap, left, right):
        for q in range(groups):
            part = slice(q * width, (q + 1) * width)
            at = pl.ds((tap * groups + q) * width, width)
            total[at, :] = dot(left[part], right[part], 1, 1)

    space_terms(slots, rows_ref, LANES // 2, store)


def final_body(factor, stride, *refs):
    (mine, *came), (space_out, time_out) = refs[:-2], refs[-2:]
    total = mine[...]
    for ref in came:
        total = total + ref[...].astype(F32)
    total = total * factor
    first, short = time_out.shape[0], space_out.shape[0] // stride
    time_out[...] = total[:first]
    for j in range(stride):
        space_out[pl.ds(j, short, stride=stride), :] = total[first + j * short : first + (j + 1) * short]


def space_body(count, *refs):
    peers = lax.axis_size("row")
    slots, refs = refs[:count], refs[count:]
    y1, c2, x2, g1, weight, x1_out, x2_out, g1_out, g2_out, rows_ref = refs
    x2_out[...] = x2[...]
    g1_out[...] = g1[...]
    me = lax.axis_index("row")
    cols, ch = y1.shape[2:]
    groups, width = weight.shape[2:4]
    rows_ref[0] = jnp.zeros(rows_ref.shape[1:], BF16)
    rows_ref[peers + 1] = jnp.zeros(rows_ref.shape[1:], BF16)
    place(slots, rows_ref, 1)
    column = lax.broadcasted_iota(jnp.int32, (LANES, width), 0) % cols
    forth, back = [None] * groups, [None] * groups
    for a in range(3):
        row = rows_ref[me + a].astype(F32).T
        for q in range(groups):
            for first, sums in ((0, forth), (ch, back)):
                value = row[:, first + q * width : first + (q + 1) * width]
                sooner = jnp.where(column == 0, 0.0, pltpu.roll(value, 1, 0))
                later = jnp.where(column == cols - 1, 0.0, pltpu.roll(value, LANES - 1, 0))
                for b, moved in enumerate((sooner, value, later)):
                    if first:
                        term = dot(moved.astype(BF16), weight[2 - a, 2 - b, q], 1, 1)
                    else:
                        term = dot(moved.astype(BF16), weight[a, b, q], 1, 0)
                    sums[q] = term if sums[q] is None else sums[q] + term
    forth = jnp.concatenate(forth, axis=-1)
    back = jnp.concatenate(back, axis=-1)
    for f in range(2):
        part = slice(f * cols, (f + 1) * cols)
        x1_out[f, 0] = (y1[f, 0].astype(F32) - forth[part]).astype(BF16)
        slope = silu_slope(x2[f, 0].astype(F32))
        g2_out[f, 0] = (c2[f, 0].astype(F32) + slope * back[part]).astype(BF16)


def swap(x, axis, bit):
    return lax.ppermute(x, axis, [(i, i ^ bit) for i in range(lax.axis_size(axis))])


def gather(x, axis, bits):
    slots = {0: x}
    for bit in reversed(bits):
        for k in list(slots):
            slots[k ^ bit] = swap(slots[k], axis, bit)
    return slots


def slot_order(peers):
    last = [k for k in range(peers) if k & 1 and k > 1]
    return [k for k in range(peers) if k not in last] + last


def row_offsets(bits):
    if not bits:
        return [0]
    rest = row_offsets(bits[1:])
    return rest + [o ^ bits[0] for o in rest]


def neighbours(x, axis, first):
    lower = range(first, lax.axis_size(axis) - 1, 2)
    return lax.ppermute(x, axis, [p for i in lower for p in ((i, i + 1), (i + 1, i))])


def per_device(y1, y2, c1, c2, weight_space, temporal_weight):
    steps, peers = lax.axis_size("tm"), lax.axis_size("row")
    devices = steps * peers
    frames, rows_here, cols, ch = y1.shape
    groups = weight_space.shape[2]
    width = ch // groups
    taps = weight_space.shape[0] * weight_space.shape[1]
    factor = 1.0 / math.sqrt(frames * rows_here * cols * devices)
    time_groups, time_width = temporal_weight.shape[1:3]
    time_rows = 3 * time_groups * time_width
    space_rows = taps * ch

    packed = on_device(open_body, (y1, c2), [shape((2 * cols, 2 * ch), BF16)], far=2)[0]
    up = [(i, i + 1) for i in range(steps - 1)]
    near, far = neighbours(packed, "tm", 0), neighbours(packed, "tm", 1)
    wide = shape((cols, 2 * ch), F32)
    centre = on_device(
        centre_body,
        (y1, y2, c1, temporal_weight, packed),
        [wide] * 3 + [shape((2, 2, cols, ch), BF16), shape(temporal_weight.shape, BF16)],
        far=4,
    )

    even = time_rows % devices == 0 and space_rows % devices == 0
    bits = [1 << i for i in range(peers.bit_length() - 1)]
    near, centre = lax.optimization_barrier((near, centre))
    early = on_device(time_near_body, (packed, near), [shape((time_rows, time_width), F32)])[0]
    if even:
        rows = time_rows // devices
        tall = round_up(rows, 16)
        offsets = row_offsets(bits[1:])
        block = (len(offsets), steps, tall, time_width)
        pieces = len(offsets)
        share = (len(offsets) * steps // pieces, *block[2:])
        kept, *sent = on_device(
            functools.partial(time_sum_body, offsets, rows),
            (packed, far, early),
            [shape(block, F32)] + [shape(share, BF16)] * pieces,
            [pltpu.VMEM((round_up(time_rows + tall, 8), time_width), F32)],
        )
        came = [swap(v, "row", 1) for v in sent]
        for bit in bits[1:]:
            block = (block[0] // 2, *block[1:])
            kept, sent = on_device(
                fold_body, (kept, *came), [shape(block, F32), shape(block, BF16)]
            )
            came = [swap(sent, "row", bit)]
    x2, g1, held = on_device(
        time_body,
        (near, far, *centre),
        [shape(y1.shape, BF16)] * 2 + [shape((2 * ch, 2 * cols), BF16)],
    )
    slots = {k: (v,) for k, v in gather(held, "row", bits[1:]).items()}
    slots[1] = (swap(held, "row", 1),)
    for k in list(slots):
        if k > 1:
            halves = (slots[k][0][:ch], slots[k][0][ch:])
            slots[k ^ 1] = tuple(swap(v, "row", 1) for v in halves)
    gathered = [v for k in slot_order(peers) for v in slots[k]]
    count = len(gathered)

    if even:
        rows = space_rows // devices
        period, layout = segments(width)
        full = -(-rows // period) * len(layout)
        deep = round_up(time_rows // devices + full, 16)
        piece = (deep, LANES)
        scratch = (round_up(space_rows + 8 * period + rows, 8), LANES)
        pieces = on_device(
            functools.partial(space_sum_body, count, groups, rows, time_rows // devices),
            gathered,
            [shape((steps, *piece), F32)],
            [pltpu.VMEM((peers, 2 * ch, 2 * cols), BF16)] + [pltpu.VMEM(scratch, F32)] * 2,
        )
        mine, *sends = on_device(
            functools.partial(join_body, time_rows // devices),
            (*pieces, kept, *came),
            [shape(piece, F32)] + [shape(piece, BF16)] * (steps - 1),
        )
        order = sorted(range(1, steps), key=lambda k: (k < steps // 2, k >= steps // 2 and k & 1, -k))
        arrived = [swap(sends[k - 1], "tm", k) for k in order]
        space_share, time_share = on_device(
            functools.partial(final_body, factor, len(layout)),
            (mine, *arrived),
            [shape((full, LANES), F32), shape((time_rows // devices, time_width), F32)],
        )
        space_share = space_share.reshape(-1)[: rows * width]
        time_share = time_share.reshape(-1)
    else:
        total = on_device(
            time_sum_whole_body, (packed, far, early), [shape((time_rows, time_width), F32)]
        )[0]
        time_share = factor * lax.psum_scatter(
            total.reshape(-1), ("tm", "row"), scatter_dimension=0, tiled=True
        )
        total = on_device(
            functools.partial(space_sum_whole_body, count, groups),
            gathered,
            [shape((space_rows, width), F32)],
            [pltpu.VMEM((peers, 2 * ch, 2 * cols), BF16)],
        )[0]
        total = total.reshape(steps, peers, -1)
        total = lax.dynamic_index_in_dim(total, lax.axis_index("row"), 1, keepdims=False)
        space_share = factor * lax.psum_scatter(
            total.reshape(-1), "tm", scatter_dimension=0, tiled=True
        )

    x1, x2, g1, g2 = on_device(
        functools.partial(space_body, count),
        (*gathered, y1, c2, x2, g1, weight_space),
        [shape(y1.shape, BF16)] * 4,
        [pltpu.VMEM((peers + 2, 2 * ch, 2 * cols), BF16)],
    )
    return x1, x2, g1, g2, space_share, time_share


def solution(mesh):
    video = P("tm", "row", None, None)
    share = P(("tm", "row"))
    return jax.shard_map(
        per_device,
        mesh=mesh,
        in_specs=(video,) * 4 + (P(), P()),
        out_specs=(video,) * 4 + (share, share),
        check_vma=False,
    )
```

```python
import functools
import math

import jax
import jax.numpy as jnp
from jax import lax
from jax.experimental import pallas as pl
from jax.experimental.pallas import tpu as pltpu
from jax.sharding import PartitionSpec as P

HAAR = 0.7071067811865476
LANES = 128
F32 = jnp.float32
BF16 = jnp.bfloat16


def round_up(value, unit):
    return (value + unit - 1) // unit * unit


def on_device(body, args, outs, scratch=(), far=0):
    whole = pl.BlockSpec(memory_space=pltpu.VMEM)
    moved = sum(math.prod(a.shape) * a.dtype.itemsize for a in (*args, *outs))
    scratch = [*scratch, *(pltpu.VMEM(a.shape, a.dtype) for a in args[:far])]
    if far:
        scratch.append(pltpu.SemaphoreType.DMA((far,)))
    return pl.pallas_call(
        body,
        out_shape=outs,
        in_specs=[pl.BlockSpec(memory_space=pltpu.HBM)] * far + [whole] * (len(args) - far),
        out_specs=[whole] * len(outs),
        scratch_shapes=scratch,
        compiler_params=pltpu.CompilerParams(vmem_limit_bytes=40 * 1024 * 1024),
        cost_estimate=pl.CostEstimate(flops=0, bytes_accessed=moved, transcendentals=0),
    )(*[pltpu.with_memory_space_constraint(a, pltpu.HBM) for a in args[:far]], *args[far:])


def shape(dims, dtype):
    return jax.ShapeDtypeStruct(tuple(dims), dtype)


def sigmoid(v):
    return 1.0 / (1.0 + jnp.exp(-v))


def silu_slope(v):
    s = sigmoid(v)
    return s * (1.0 + v * (1.0 - s))


def dot(left, right, left_dim, right_dim):
    return lax.dot_general(
        left, right, (((left_dim,), (right_dim,)), ((), ())), preferred_element_type=F32
    )


def squeezed(ref):
    even, odd = ref[0, 0].astype(F32), ref[1, 0].astype(F32)
    return jnp.concatenate([(even + odd) * HAAR, (even - odd) * HAAR], axis=-1)


def unsqueezed(packed):
    half = packed.shape[-1] // 2
    low, high = packed[:, :half], packed[:, half:]
    return (low + high) * HAAR, (low - high) * HAAR


def fetch(far, near, sems):
    copies = [pltpu.make_async_copy(f, n, sems.at[i]) for i, (f, n) in enumerate(zip(far, near))]
    for copy in copies:
        copy.start()
    for copy in copies:
        copy.wait()


def open_body(y_far, cot_far, out_ref, y_ref, cot_ref, sems):
    fetch((y_far, cot_far), (y_ref, cot_ref), sems)
    sq = squeezed(y_ref)
    cols = sq.shape[0]
    out_ref[:cols] = (sq * sigmoid(sq)).astype(BF16)
    out_ref[cols:] = squeezed(cot_ref).astype(BF16)


def centre_body(y1_far, y2_far, c1_far, weight_far, own, *refs):
    (forth, back, slope, base, weight_out), (y1, y2, c1, weight, sems) = refs[:5], refs[5:]
    fetch((y1_far, y2_far, c1_far, weight_far), (y1, y2, c1, weight), sems)
    cols = own.shape[0] // 2
    groups, width = weight.shape[1:3]
    for q in range(groups):
        lanes = slice(q * width, (q + 1) * width)
        forth[:, lanes] = dot(own[:cols, lanes], weight[1, q], 1, 0)
        back[:, lanes] = dot(own[cols:, lanes], weight[1, q], 1, 1)
    slope[...] = silu_slope(squeezed(y1))
    for f in range(2):
        base[0, f] = y2[f, 0]
        base[1, f] = c1[f, 0]
    weight_out[...] = weight[...]


def time_body(near, far, forth0, back0, slope, base, weight, x2_out, g1_out, held_out):
    cols = forth0.shape[0]
    groups, width = weight.shape[1:3]
    tap = jnp.where(lax.axis_index("tm") % 2 == 0, 2, 0)
    forth, back = [], []
    for q in range(groups):
        lanes = slice(q * width, (q + 1) * width)
        forth.append(
            forth0[:, lanes]
            + dot(near[:cols, lanes], weight[tap, q], 1, 0)
            + dot(far[:cols, lanes], weight[2 - tap, q], 1, 0)
        )
        back.append(
            back0[:, lanes]
            + dot(near[cols:, lanes], weight[2 - tap, q], 1, 1)
            + dot(far[cols:, lanes], weight[tap, q], 1, 1)
        )
    branch = unsqueezed(jnp.concatenate(forth, axis=-1))
    back = unsqueezed(jnp.concatenate(back, axis=-1) * slope[...])
    acts, cots = [], []
    for f in range(2):
        x2 = (base[0, f].astype(F32) - branch[f].astype(BF16).astype(F32)).astype(BF16)
        g1 = (base[1, f].astype(F32) + back[f].astype(BF16).astype(F32)).astype(BF16)
        x2_out[f, 0] = x2
        g1_out[f, 0] = g1
        v = x2.astype(F32)
        acts.append(v * sigmoid(v))
        cots.append(g1.astype(F32))
    ch = held_out.shape[0] // 2
    held_out[:ch] = jnp.concatenate(acts, axis=0).T.astype(BF16)
    held_out[ch:] = jnp.concatenate(cots, axis=0).T.astype(BF16)


def time_terms(own, pairs, total):
    cols = own.shape[0] // 2
    width = total.shape[1]
    groups = own.shape[1] // width
    act = own[:cols].astype(F32).T.astype(BF16)
    for k, cot in pairs:
        for q in range(groups):
            part = slice(q * width, (q + 1) * width)
            at = pl.multiple_of((k * groups + q) * width, width)
            total[pl.ds(at, width), :] = dot(act[part], cot[cols:, part], 1, 0)


def near_tap():
    return jnp.where(lax.axis_index("tm") % 2 == 0, 0, 2)


def time_near_body(near, *refs):
    owns, total = refs[:-1], refs[-1]
    cols = near.shape[0] // 2
    width = total.shape[1]
    groups = near.shape[1] // width
    total[...] = jnp.zeros_like(total)
    time_terms(owns[0], ((near_tap(), near),), total)
    act = jnp.concatenate([v[:cols] for v in owns], axis=0).astype(F32).T.astype(BF16)
    cot = jnp.concatenate([v[cols:] for v in owns], axis=0)
    for q in range(groups):
        part = slice(q * width, (q + 1) * width)
        total[pl.ds((groups + q) * width, width), :] = dot(act[part], cot[:, part], 1, 0)


def outer_steps(steps, peers, taps, rows):
    size = steps * peers * rows // taps
    return [
        t
        for t in range(steps)
        if t * peers * rows < size or (t + 1) * peers * rows > (taps - 1) * size
    ]


def time_sum_body(offsets, rows, own, far, early, keep, *refs):
    sends, total = refs[:-1], refs[-1]
    total[: early.shape[0]] = early[...]
    time_terms(own, ((2 - near_tap(), far),), total)
    me, peers, steps = lax.axis_index("row"), lax.axis_size("row"), lax.axis_size("tm")
    held, third = keep.shape[2], early.shape[0] // 3
    for u, offset in enumerate(offsets):
        if u == 1:
            total[third : 2 * third] = jnp.zeros((third, total.shape[1]), F32)
        for i, t in enumerate(range(steps) if u == 0 else outer_steps(steps, peers, 3, rows)):
            mine = (t * peers + (me ^ offset)) * rows
            other = (t * peers + (me ^ offset ^ 1)) * rows
            keep[u, i] = total[pl.ds(mine, held), :]
            sends[u][i] = total[pl.ds(other, held), :].astype(BF16)


def time_sum_whole_body(own, far, early, total):
    total[...] = early[...]
    time_terms(own, ((2 - near_tap(), far),), total)


def fold_body(kept, own_came, other_came, keep, send):
    keep[...] = kept[0] + own_came[...].astype(F32)
    send[...] = (kept[1, : send.shape[0]] + other_came[...].astype(F32)).astype(BF16)


def place(slots, rows_ref, lead):
    me, ch = lax.axis_index("row"), rows_ref.shape[1]
    peers = lax.axis_size("row")
    whole = peers // 2 + 1
    rest = slots[whole:]
    parts = len(rest) // (peers - whole) if rest else 1
    slots = [(v,) for v in slots[:whole]] + [
        rest[i : i + parts] for i in range(0, len(rest), parts)
    ]
    for k, refs in zip(slot_order(peers), slots):
        for j, ref in enumerate(refs):
            size = ch // len(refs)
            rows_ref[(me ^ k) + lead, j * size : (j + 1) * size] = ref[...]


def space_terms(slots, rows_ref, cols, store):
    peers = lax.axis_size("row")
    ch = rows_ref.shape[1] // 2
    place(slots, rows_ref, 0)
    column = lax.broadcasted_iota(jnp.int32, (ch, LANES), 1) % cols
    act, shifts = [], ([], [], [])
    for r in range(peers):
        act.append(rows_ref[r, :ch])
        cot = rows_ref[r, ch:]
        wide = cot.astype(F32)
        later = jnp.where(column == cols - 1, 0.0, pltpu.roll(wide, LANES - 1, 1))
        sooner = jnp.where(column == 0, 0.0, pltpu.roll(wide, 1, 1))
        for held, value in zip(shifts, (later.astype(BF16), cot, sooner.astype(BF16))):
            held.append(value)
    for a in range(3):
        pairs = [(r, r - a + 1) for r in range(peers) if 0 <= r - a + 1 < peers]
        left = jnp.concatenate([act[r] for r, _ in pairs], axis=1)
        for b in range(3):
            right = jnp.concatenate([shifts[b][r] for _, r in pairs], axis=1)
            store(a * 3 + b, left, right)


def segments(width):
    period = LANES // math.gcd(width, LANES)
    found = []
    for j in range(period * width // LANES):
        row, lane = [], 0
        while lane < LANES:
            at = j * LANES + lane
            source, column = divmod(at, width)
            tile, first = divmod(column, LANES)
            row.append((lane, source, tile, (lane - first) % LANES))
            lane += min(LANES - first, width - column, LANES - lane)
        found.append(row)
    return period, found


def space_sum_body(count, groups, rows, time_rows, *refs):
    peers, steps = lax.axis_size("row"), lax.axis_size("tm")
    slots, refs = refs[:count], refs[count:]
    out, rows_ref, main, rest = refs
    ch = rows_ref.shape[1] // 2
    width = ch // groups

    def store(tap, left, right):
        for q in range(groups):
            part = slice(q * width, (q + 1) * width)
            term = dot(left[part], right[part], 1, 1)
            at = pl.ds((tap * groups + q) * width, width)
            main[at, :] = term[:, :LANES]
            rest[at, : width - LANES] = term[:, LANES:]

    space_terms(slots, rows_ref, LANES // 2, store)
    period, layout = segments(width)
    held = round_up(-(-rows // period), 8)
    lane = lax.broadcasted_iota(jnp.int32, (held, LANES), 1)
    here, me = lax.axis_index("tm"), lax.axis_index("row")
    short = -(-rows // period)
    for k in range(steps):
        t = here ^ k
        start = (t * peers + me) * rows
        rolled = {}

        def source(j, tile, amount):
            if (j, tile, amount) not in rolled:
                ref = (main, rest)[tile]
                value = ref[pl.ds(start + j, held, stride=period), :]
                rolled[j, tile, amount] = pltpu.roll(value, amount, 1) if amount else value
            return rolled[j, tile, amount]

        parts = [jnp.zeros((time_rows, LANES), F32)]
        for row in layout:
            value = None
            for first, j, tile, amount in row:
                piece = source(j, tile, amount)
                value = piece if value is None else jnp.where(lane < first, value, piece)
            parts.append(value[:short])
        blank = out.shape[1] - time_rows - short * len(layout)
        if blank:
            parts.append(jnp.zeros((blank, LANES), F32))
        out[k] = jnp.concatenate(parts, axis=0)


def join_body(time_rows, outer, pieces, kept, came, mine, *sends):
    tall, steps = kept.shape[1], kept.shape[0]
    row = lax.broadcasted_iota(jnp.int32, (tall, LANES), 0)
    gap = steps - len(outer)
    for k in range(pieces.shape[0]):
        t = lax.axis_index("tm") ^ k
        first = next((i for i, v in enumerate(outer) if v != i), len(outer))
        over = t >= first + gap
        sent = jnp.logical_or(t < first, over)
        terms = came[jnp.where(over, t - gap, jnp.minimum(t, len(outer) - 1))].astype(F32)
        terms = kept[t] + jnp.where(sent, terms, 0.0)
        head = pieces[k, :tall] + jnp.where(row < time_rows, terms, 0.0)
        piece = jnp.concatenate([head, pieces[k, tall:]], axis=0)
        if k == 0:
            mine[...] = piece
        else:
            sends[k - 1][...] = piece.astype(BF16)


def space_sum_whole_body(count, groups, *refs):
    slots, (total, rows_ref) = refs[:count], refs[count:]
    ch = rows_ref.shape[1] // 2
    width = ch // groups

    def store(tap, left, right):
        for q in range(groups):
            part = slice(q * width, (q + 1) * width)
            at = pl.ds((tap * groups + q) * width, width)
            total[at, :] = dot(left[part], right[part], 1, 1)

    space_terms(slots, rows_ref, LANES // 2, store)


def final_body(factor, stride, *refs):
    (mine, *came), (space_out, time_out) = refs[:-2], refs[-2:]
    total = mine[...]
    for ref in came:
        total = total + ref[...].astype(F32)
    total = total * factor
    first, short = time_out.shape[0], space_out.shape[0] // stride
    time_out[...] = total[:first]
    for j in range(stride):
        space_out[pl.ds(j, short, stride=stride), :] = total[first + j * short : first + (j + 1) * short]


def space_body(count, *refs):
    peers = lax.axis_size("row")
    slots, refs = refs[:count], refs[count:]
    y1, c2, x2, g1, weight, x1_out, x2_out, g1_out, g2_out, rows_ref = refs
    x2_out[...] = x2[...]
    g1_out[...] = g1[...]
    me = lax.axis_index("row")
    cols, ch = y1.shape[2:]
    groups, width = weight.shape[2:4]
    rows_ref[0] = jnp.zeros(rows_ref.shape[1:], BF16)
    rows_ref[peers + 1] = jnp.zeros(rows_ref.shape[1:], BF16)
    place(slots, rows_ref, 1)
    column = lax.broadcasted_iota(jnp.int32, (LANES, width), 0) % cols
    forth, back = [None] * groups, [None] * groups
    for a in range(3):
        row = rows_ref[me + a].astype(F32).T
        for q in range(groups):
            for first, sums in ((0, forth), (ch, back)):
                value = row[:, first + q * width : first + (q + 1) * width]
                sooner = jnp.where(column == 0, 0.0, pltpu.roll(value, 1, 0))
                later = jnp.where(column == cols - 1, 0.0, pltpu.roll(value, LANES - 1, 0))
                for b, moved in enumerate((sooner, value, later)):
                    if first:
                        term = dot(moved.astype(BF16), weight[2 - a, 2 - b, q], 1, 1)
                    else:
                        term = dot(moved.astype(BF16), weight[a, b, q], 1, 0)
                    sums[q] = term if sums[q] is None else sums[q] + term
    forth = jnp.concatenate(forth, axis=-1)
    back = jnp.concatenate(back, axis=-1)
    for f in range(2):
        part = slice(f * cols, (f + 1) * cols)
        x1_out[f, 0] = (y1[f, 0].astype(F32) - forth[part]).astype(BF16)
        slope = silu_slope(x2[f, 0].astype(F32))
        g2_out[f, 0] = (c2[f, 0].astype(F32) + slope * back[part]).astype(BF16)


def swap(x, axis, bit):
    return lax.ppermute(x, axis, [(i, i ^ bit) for i in range(lax.axis_size(axis))])


def gather(x, axis, bits):
    slots = {0: x}
    for bit in reversed(bits):
        for k in list(slots):
            slots[k ^ bit] = swap(slots[k], axis, bit)
    return slots


def slot_order(peers):
    last = [k for k in range(peers) if k & 1 and k > 1]
    return [k for k in range(peers) if k not in last] + last


def row_offsets(bits):
    if not bits:
        return [0]
    rest = row_offsets(bits[1:])
    return rest + [o ^ bits[0] for o in rest]


def neighbours(x, axis, first):
    lower = range(first, lax.axis_size(axis) - 1, 2)
    return lax.ppermute(x, axis, [p for i in lower for p in ((i, i + 1), (i + 1, i))])


def per_device(y1, y2, c1, c2, weight_space, temporal_weight):
    steps, peers = lax.axis_size("tm"), lax.axis_size("row")
    devices = steps * peers
    frames, rows_here, cols, ch = y1.shape
    groups = weight_space.shape[2]
    width = ch // groups
    taps = weight_space.shape[0] * weight_space.shape[1]
    factor = 1.0 / math.sqrt(frames * rows_here * cols * devices)
    time_groups, time_width = temporal_weight.shape[1:3]
    time_rows = 3 * time_groups * time_width
    space_rows = taps * ch

    packed = on_device(open_body, (y1, c2), [shape((2 * cols, 2 * ch), BF16)], far=2)[0]
    up = [(i, i + 1) for i in range(steps - 1)]
    near, far = neighbours(packed, "tm", 0), neighbours(packed, "tm", 1)
    wide = shape((cols, 2 * ch), F32)
    centre = on_device(
        centre_body,
        (y1, y2, c1, temporal_weight, packed),
        [wide] * 3 + [shape((2, 2, cols, ch), BF16), shape(temporal_weight.shape, BF16)],
        far=4,
    )

    near, centre = lax.optimization_barrier((near, centre))
    bits = [1 << i for i in range(peers.bit_length() - 1)]
    even = time_rows % devices == 0 and space_rows % devices == 0 and peers == 4
    owns = gather(packed, "row", bits[1:]) if even else {0: packed}
    owns = [owns[k] for k in sorted(owns)]
    early = on_device(time_near_body, (near, *owns), [shape((time_rows, time_width), F32)])[0]
    if even:
        rows = time_rows // devices
        tall = round_up(rows, 16)
        offsets = row_offsets(bits[1:])
        block = (steps, tall, time_width)
        outer = outer_steps(steps, peers, 3, rows)
        rest = (len(outer), *block[1:])
        kept, *sent = on_device(
            functools.partial(time_sum_body, offsets, rows),
            (packed, far, early),
            [shape((2, *block), F32), shape(block, BF16), shape(rest, BF16)],
            [pltpu.VMEM((round_up(time_rows + tall, 8), time_width), F32)],
        )
        came = [swap(v, "row", 1) for v in sent]
        kept, sent = on_device(fold_body, (kept, *came), [shape(block, F32), shape(rest, BF16)])
        came = [swap(sent, "row", bits[1])]
    x2, g1, held = on_device(
        time_body,
        (near, far, *centre),
        [shape(y1.shape, BF16)] * 2 + [shape((2 * ch, 2 * cols), BF16)],
    )
    slots = {k: (v,) for k, v in gather(held, "row", bits[1:]).items()}
    slots[1] = (swap(held, "row", 1),)
    for k in list(slots):
        if k > 1:
            halves = (slots[k][0][:ch], slots[k][0][ch:])
            slots[k ^ 1] = tuple(swap(v, "row", 1) for v in halves)
    gathered = [v for k in slot_order(peers) for v in slots[k]]
    count = len(gathered)

    if even:
        rows = space_rows // devices
        period, layout = segments(width)
        full = -(-rows // period) * len(layout)
        deep = round_up(time_rows // devices + full, 16)
        piece = (deep, LANES)
        scratch = (round_up(space_rows + 8 * period + rows, 8), LANES)
        pieces = on_device(
            functools.partial(space_sum_body, count, groups, rows, time_rows // devices),
            gathered,
            [shape((steps, *piece), F32)],
            [pltpu.VMEM((peers, 2 * ch, 2 * cols), BF16)] + [pltpu.VMEM(scratch, F32)] * 2,
        )
        mine, *sends = on_device(
            functools.partial(join_body, time_rows // devices, outer),
            (*pieces, kept, *came),
            [shape(piece, F32)] + [shape(piece, BF16)] * (steps - 1),
        )
        order = sorted(range(1, steps), key=lambda k: (k < steps // 2, k >= steps // 2 and k & 1, -k))
        arrived = [swap(sends[k - 1], "tm", k) for k in order]
        space_share, time_share = on_device(
            functools.partial(final_body, factor, len(layout)),
            (mine, *arrived),
            [shape((full, LANES), F32), shape((time_rows // devices, time_width), F32)],
        )
        space_share = space_share.reshape(-1)[: rows * width]
        time_share = time_share.reshape(-1)
    else:
        total = on_device(
            time_sum_whole_body, (packed, far, early), [shape((time_rows, time_width), F32)]
        )[0]
        time_share = factor * lax.psum_scatter(
            total.reshape(-1), ("tm", "row"), scatter_dimension=0, tiled=True
        )
        total = on_device(
            functools.partial(space_sum_whole_body, count, groups),
            gathered,
            [shape((space_rows, width), F32)],
            [pltpu.VMEM((peers, 2 * ch, 2 * cols), BF16)],
        )[0]
        total = total.reshape(steps, peers, -1)
        total = lax.dynamic_index_in_dim(total, lax.axis_index("row"), 1, keepdims=False)
        space_share = factor * lax.psum_scatter(
            total.reshape(-1), "tm", scatter_dimension=0, tiled=True
        )

    x1, x2, g1, g2 = on_device(
        functools.partial(space_body, count),
        (*gathered, y1, c2, x2, g1, weight_space),
        [shape(y1.shape, BF16)] * 4,
        [pltpu.VMEM((peers + 2, 2 * ch, 2 * cols), BF16)],
    )
    return x1, x2, g1, g2, space_share, time_share


def solution(mesh):
    video = P("tm", "row", None, None)
    share = P(("tm", "row"))
    return jax.shard_map(
        per_device,
        mesh=mesh,
        in_specs=(video,) * 4 + (P(), P()),
        out_specs=(video,) * 4 + (share, share),
        check_vma=False,
    )
```

```python
import functools
import math

import jax
import jax.numpy as jnp
from jax import lax
from jax.experimental import pallas as pl
from jax.experimental.pallas import tpu as pltpu
from jax.sharding import PartitionSpec as P

HAAR = 0.7071067811865476
LANES = 128
F32 = jnp.float32
BF16 = jnp.bfloat16


def round_up(value, unit):
    return (value + unit - 1) // unit * unit


def on_device(body, args, outs, scratch=(), far=0):
    whole = pl.BlockSpec(memory_space=pltpu.VMEM)
    moved = sum(math.prod(a.shape) * a.dtype.itemsize for a in (*args, *outs))
    scratch = [*scratch, *(pltpu.VMEM(a.shape, a.dtype) for a in args[:far])]
    if far:
        scratch.append(pltpu.SemaphoreType.DMA((far,)))
    return pl.pallas_call(
        body,
        out_shape=outs,
        in_specs=[pl.BlockSpec(memory_space=pltpu.HBM)] * far + [whole] * (len(args) - far),
        out_specs=[whole] * len(outs),
        scratch_shapes=scratch,
        compiler_params=pltpu.CompilerParams(vmem_limit_bytes=40 * 1024 * 1024),
        cost_estimate=pl.CostEstimate(flops=0, bytes_accessed=moved, transcendentals=0),
    )(*[pltpu.with_memory_space_constraint(a, pltpu.HBM) for a in args[:far]], *args[far:])


def shape(dims, dtype):
    return jax.ShapeDtypeStruct(tuple(dims), dtype)


def sigmoid(v):
    return 1.0 / (1.0 + jnp.exp(-v))


def silu_slope(v):
    s = sigmoid(v)
    return s * (1.0 + v * (1.0 - s))


def dot(left, right, left_dim, right_dim):
    return lax.dot_general(
        left, right, (((left_dim,), (right_dim,)), ((), ())), preferred_element_type=F32
    )


def squeezed(ref):
    even, odd = ref[0, 0].astype(F32), ref[1, 0].astype(F32)
    return jnp.concatenate([(even + odd) * HAAR, (even - odd) * HAAR], axis=-1)


def unsqueezed(packed):
    half = packed.shape[-1] // 2
    low, high = packed[:, :half], packed[:, half:]
    return (low + high) * HAAR, (low - high) * HAAR


def fetch(far, near, sems):
    copies = [pltpu.make_async_copy(f, n, sems.at[i]) for i, (f, n) in enumerate(zip(far, near))]
    for copy in copies:
        copy.start()
    for copy in copies:
        copy.wait()


def open_body(y_far, cot_far, out_ref, y_ref, cot_ref, sems):
    fetch((y_far, cot_far), (y_ref, cot_ref), sems)
    sq = squeezed(y_ref)
    cols = sq.shape[0]
    out_ref[:cols] = (sq * sigmoid(sq)).astype(BF16)
    out_ref[cols:] = squeezed(cot_ref).astype(BF16)


def centre_body(y1_far, y2_far, c1_far, weight_far, own, *refs):
    (forth, back, slope, base, weight_out), (y1, y2, c1, weight, sems) = refs[:5], refs[5:]
    fetch((y1_far, y2_far, c1_far, weight_far), (y1, y2, c1, weight), sems)
    cols = own.shape[0] // 2
    groups, width = weight.shape[1:3]
    for q in range(groups):
        lanes = slice(q * width, (q + 1) * width)
        forth[:, lanes] = dot(own[:cols, lanes], weight[1, q], 1, 0)
        back[:, lanes] = dot(own[cols:, lanes], weight[1, q], 1, 1)
    slope[...] = silu_slope(squeezed(y1))
    for f in range(2):
        base[0, f] = y2[f, 0]
        base[1, f] = c1[f, 0]
    weight_out[...] = weight[...]


def time_body(near, near_cot, far, forth0, back0, slope, base, weight, x2_out, g1_out, held_out):
    cols = forth0.shape[0]
    groups, width = weight.shape[1:3]
    tap = jnp.where(lax.axis_index("tm") % 2 == 0, 2, 0)
    forth, back = [], []
    for q in range(groups):
        lanes = slice(q * width, (q + 1) * width)
        sides = jnp.concatenate([near[:cols, lanes], far[:cols, lanes]], axis=1)
        taps = jnp.concatenate([weight[tap, q], weight[2 - tap, q]], axis=0)
        forth.append(forth0[:, lanes] + dot(sides, taps, 1, 0))
        sides = jnp.concatenate([near_cot[:, lanes], far[cols:, lanes]], axis=1)
        taps = jnp.concatenate([weight[2 - tap, q], weight[tap, q]], axis=1)
        back.append(back0[:, lanes] + dot(sides, taps, 1, 1))
    branch = unsqueezed(jnp.concatenate(forth, axis=-1))
    back = unsqueezed(jnp.concatenate(back, axis=-1) * slope[...])
    acts, cots = [], []
    for f in range(2):
        x2 = (base[0, f].astype(F32) - branch[f].astype(BF16).astype(F32)).astype(BF16)
        g1 = (base[1, f].astype(F32) + back[f].astype(BF16).astype(F32)).astype(BF16)
        x2_out[f, 0] = x2
        g1_out[f, 0] = g1
        v = x2.astype(F32)
        acts.append(v * sigmoid(v))
        cots.append(g1.astype(F32))
    ch = held_out.shape[0] // 2
    held_out[:ch] = jnp.concatenate(acts, axis=0).astype(BF16).T
    held_out[ch:] = jnp.concatenate(cots, axis=0).astype(BF16).T


def time_terms(near_cot, far, owns, total):
    cols = far.shape[0] // 2
    width = total.shape[1]
    groups = far.shape[1] // width
    act = jnp.concatenate([v[:cols] for v in owns], axis=0).T
    own = jnp.concatenate([v[cols:] for v in owns], axis=0)
    tap = jnp.where(lax.axis_index("tm") % 2 == 0, 0, 2)
    for k, cot in ((1, own), (tap, near_cot[...]), (2 - tap, far[cols:])):
        for q in range(groups):
            part = slice(q * width, (q + 1) * width)
            at = pl.multiple_of((k * groups + q) * width, width)
            total[pl.ds(at, width), :] = dot(act[part, : cot.shape[0]], cot[:, part], 1, 0)


def outer_steps(steps, peers, taps, rows):
    size = steps * peers * rows // taps
    return [
        t
        for t in range(steps)
        if t * peers * rows < size or (t + 1) * peers * rows > (taps - 1) * size
    ]


def time_sum_body(offsets, rows, near_cot, far, *refs):
    owns, refs, total = refs[: len(offsets)], refs[len(offsets) : -1], refs[-1]
    keeps, sends = refs[: len(offsets)], refs[len(offsets) :]
    time_terms(near_cot, far, owns, total)
    me, peers, steps = lax.axis_index("row"), lax.axis_size("row"), lax.axis_size("tm")
    held, third = keeps[0].shape[1], steps * peers * rows // 3
    for u, offset in enumerate(offsets):
        if u == 1:
            total[third : 2 * third] = jnp.zeros((third, total.shape[1]), F32)
        for i, t in enumerate(range(steps) if u == 0 else outer_steps(steps, peers, 3, rows)):
            mine = (t * peers + (me ^ offset)) * rows
            other = (t * peers + (me ^ offset ^ 1)) * rows
            keeps[u][i] = total[pl.ds(mine, held), :]
            sends[u][i] = total[pl.ds(other, held), :].astype(BF16)


def time_sum_whole_body(near_cot, far, own, total):
    time_terms(near_cot, far, (own,), total)


def fold_body(kept, came, send):
    send[...] = (kept[...] + came[...].astype(F32)).astype(BF16)


def place(slots, rows_ref, lead):
    me, ch = lax.axis_index("row"), rows_ref.shape[1]
    peers = lax.axis_size("row")
    whole = peers // 2 + 1
    rest = slots[whole:]
    parts = len(rest) // (peers - whole) if rest else 1
    slots = [(v,) for v in slots[:whole]] + [
        rest[i : i + parts] for i in range(0, len(rest), parts)
    ]
    for k, refs in zip(slot_order(peers), slots):
        for j, ref in enumerate(refs):
            size = ch // len(refs)
            rows_ref[(me ^ k) + lead, j * size : (j + 1) * size] = ref[...]


def space_terms(slots, rows_ref, cols, store):
    peers = lax.axis_size("row")
    ch = rows_ref.shape[1] // 2
    place(slots, rows_ref, 0)
    column = lax.broadcasted_iota(jnp.int32, (ch, LANES), 1) % cols
    act, shifts = [], ([], [], [])
    for r in range(peers):
        act.append(rows_ref[r, :ch])
        cot = rows_ref[r, ch:]
        wide = cot.astype(F32)
        later = jnp.where(column == cols - 1, 0.0, pltpu.roll(wide, LANES - 1, 1))
        sooner = jnp.where(column == 0, 0.0, pltpu.roll(wide, 1, 1))
        for held, value in zip(shifts, (later.astype(BF16), cot, sooner.astype(BF16))):
            held.append(value)
    for a in range(3):
        pairs = [(r, r - a + 1) for r in range(peers) if 0 <= r - a + 1 < peers]
        left = jnp.concatenate([act[r] for r, _ in pairs], axis=1)
        for b in range(3):
            right = jnp.concatenate([shifts[b][r] for _, r in pairs], axis=1)
            store(a * 3 + b, left, right)


def segments(width):
    period = LANES // math.gcd(width, LANES)
    found = []
    for j in range(period * width // LANES):
        row, lane = [], 0
        while lane < LANES:
            at = j * LANES + lane
            source, column = divmod(at, width)
            tile, first = divmod(column, LANES)
            row.append((lane, source, tile, (lane - first) % LANES))
            lane += min(LANES - first, width - column, LANES - lane)
        found.append(row)
    return period, found


def space_sum_body(count, groups, rows, time_rows, *refs):
    peers, steps = lax.axis_size("row"), lax.axis_size("tm")
    slots, refs = refs[:count], refs[count:]
    out, rows_ref, main, rest = refs
    ch = rows_ref.shape[1] // 2
    width = ch // groups

    def store(tap, left, right):
        for q in range(groups):
            part = slice(q * width, (q + 1) * width)
            term = dot(left[part], right[part], 1, 1)
            at = pl.ds((tap * groups + q) * width, width)
            main[at, :] = term[:, :LANES]
            rest[at, : width - LANES] = term[:, LANES:]

    space_terms(slots, rows_ref, LANES // 2, store)
    period, layout = segments(width)
    held = round_up(-(-rows // period), 8)
    lane = lax.broadcasted_iota(jnp.int32, (held, LANES), 1)
    here, me = lax.axis_index("tm"), lax.axis_index("row")
    short = -(-rows // period)
    for k in range(steps):
        t = here ^ k
        start = (t * peers + me) * rows
        rolled = {}

        def source(j, tile, amount):
            if (j, tile, amount) not in rolled:
                ref = (main, rest)[tile]
                value = ref[pl.ds(start + j, held, stride=period), :]
                rolled[j, tile, amount] = pltpu.roll(value, amount, 1) if amount else value
            return rolled[j, tile, amount]

        parts = [jnp.zeros((time_rows, LANES), F32)]
        for row in layout:
            value = None
            for first, j, tile, amount in row:
                piece = source(j, tile, amount)
                value = piece if value is None else jnp.where(lane < first, value, piece)
            parts.append(value[:short])
        blank = out.shape[1] - time_rows - short * len(layout)
        if blank:
            parts.append(jnp.zeros((blank, LANES), F32))
        out[k] = jnp.concatenate(parts, axis=0)


def join_body(time_rows, outer, pieces, kept, core_came, came, mine, *sends):
    tall, steps = kept.shape[1], kept.shape[0]
    row = lax.broadcasted_iota(jnp.int32, (tall, LANES), 0)
    gap = steps - len(outer)
    for k in range(pieces.shape[0]):
        t = lax.axis_index("tm") ^ k
        first = next((i for i, v in enumerate(outer) if v != i), len(outer))
        over = t >= first + gap
        sent = jnp.logical_or(t < first, over)
        terms = came[jnp.where(over, t - gap, jnp.minimum(t, len(outer) - 1))].astype(F32)
        terms = kept[t] + core_came[t].astype(F32) + jnp.where(sent, terms, 0.0)
        head = pieces[k, :tall] + jnp.where(row < time_rows, terms, 0.0)
        piece = jnp.concatenate([head, pieces[k, tall:]], axis=0)
        if k == 0:
            mine[...] = piece
        else:
            sends[k - 1][...] = piece.astype(BF16)


def space_sum_whole_body(count, groups, *refs):
    slots, (total, rows_ref) = refs[:count], refs[count:]
    ch = rows_ref.shape[1] // 2
    width = ch // groups

    def store(tap, left, right):
        for q in range(groups):
            part = slice(q * width, (q + 1) * width)
            at = pl.ds((tap * groups + q) * width, width)
            total[at, :] = dot(left[part], right[part], 1, 1)

    space_terms(slots, rows_ref, LANES // 2, store)


def final_body(factor, stride, *refs):
    (mine, *came), (space_out, time_out) = refs[:-2], refs[-2:]
    total = mine[...]
    for ref in came:
        total = total + ref[...].astype(F32)
    total = total * factor
    first, short = time_out.shape[0], space_out.shape[0] // stride
    time_out[...] = total[:first]
    for j in range(stride):
        space_out[pl.ds(j, short, stride=stride), :] = total[first + j * short : first + (j + 1) * short]


def space_body(count, *refs):
    peers = lax.axis_size("row")
    slots, refs = refs[:count], refs[count:]
    y1, c2, x2, g1, weight, x1_out, x2_out, g1_out, g2_out, rows_ref = refs
    x2_out[...] = x2[...]
    g1_out[...] = g1[...]
    me = lax.axis_index("row")
    cols, ch = y1.shape[2:]
    groups, width = weight.shape[2:4]
    rows_ref[0] = jnp.zeros(rows_ref.shape[1:], BF16)
    rows_ref[peers + 1] = jnp.zeros(rows_ref.shape[1:], BF16)
    place(slots, rows_ref, 1)
    column = lax.broadcasted_iota(jnp.int32, (LANES, width), 0) % cols
    forth, back = [None] * groups, [None] * groups
    for a in range(3):
        row = rows_ref[me + a].astype(F32).T
        for q in range(groups):
            for first, sums in ((0, forth), (ch, back)):
                value = row[:, first + q * width : first + (q + 1) * width]
                sooner = jnp.where(column == 0, 0.0, pltpu.roll(value, 1, 0))
                later = jnp.where(column == cols - 1, 0.0, pltpu.roll(value, LANES - 1, 0))
                for b, moved in enumerate((sooner, value, later)):
                    if first:
                        term = dot(moved.astype(BF16), weight[2 - a, 2 - b, q], 1, 1)
                    else:
                        term = dot(moved.astype(BF16), weight[a, b, q], 1, 0)
                    sums[q] = term if sums[q] is None else sums[q] + term
    forth = jnp.concatenate(forth, axis=-1)
    back = jnp.concatenate(back, axis=-1)
    for f in range(2):
        part = slice(f * cols, (f + 1) * cols)
        x1_out[f, 0] = (y1[f, 0].astype(F32) - forth[part]).astype(BF16)
        slope = silu_slope(x2[f, 0].astype(F32))
        g2_out[f, 0] = (c2[f, 0].astype(F32) + slope * back[part]).astype(BF16)


def swap(x, axis, bit):
    return lax.ppermute(x, axis, [(i, i ^ bit) for i in range(lax.axis_size(axis))])


def gather(x, axis, bits):
    slots = {0: x}
    for bit in reversed(bits):
        for k in list(slots):
            slots[k ^ bit] = swap(slots[k], axis, bit)
    return slots


def slot_order(peers):
    last = [k for k in range(peers) if k & 1 and k > 1]
    return [k for k in range(peers) if k not in last] + last


def row_offsets(bits):
    if not bits:
        return [0]
    rest = row_offsets(bits[1:])
    return rest + [o ^ bits[0] for o in rest]


def neighbours(x, axis, first):
    lower = range(first, lax.axis_size(axis) - 1, 2)
    return lax.ppermute(x, axis, [p for i in lower for p in ((i, i + 1), (i + 1, i))])


def per_device(y1, y2, c1, c2, weight_space, temporal_weight):
    steps, peers = lax.axis_size("tm"), lax.axis_size("row")
    devices = steps * peers
    frames, rows_here, cols, ch = y1.shape
    groups = weight_space.shape[2]
    width = ch // groups
    taps = weight_space.shape[0] * weight_space.shape[1]
    factor = 1.0 / math.sqrt(frames * rows_here * cols * devices)
    time_groups, time_width = temporal_weight.shape[1:3]
    time_rows = 3 * time_groups * time_width
    space_rows = taps * ch

    packed = on_device(open_body, (y1, c2), [shape((2 * cols, 2 * ch), BF16)], far=2)[0]
    up = [(i, i + 1) for i in range(steps - 1)]
    near, far = neighbours(packed, "tm", 0), neighbours(packed, "tm", 1)
    wide = shape((cols, 2 * ch), F32)
    centre = on_device(
        centre_body,
        (y1, y2, c1, temporal_weight, packed),
        [wide] * 3 + [shape((2, 2, cols, ch), BF16), shape(temporal_weight.shape, BF16)],
        far=4,
    )

    near, centre = lax.optimization_barrier((near, centre))
    near_cot = near[cols:]
    bits = [1 << i for i in range(peers.bit_length() - 1)]
    even = time_rows % devices == 0 and space_rows % devices == 0 and peers == 4
    owns = gather(packed, "row", bits[1:]) if even else {0: packed}
    owns = [owns[k] for k in sorted(owns)]
    if even:
        rows = time_rows // devices
        tall = round_up(rows, 16)
        offsets = row_offsets(bits[1:])
        block = (steps, tall, time_width)
        outer = outer_steps(steps, peers, 3, rows)
        rest = (len(outer), *block[1:])
        kept, other, sent_own, core_sent = on_device(
            functools.partial(time_sum_body, offsets, rows),
            (near_cot, far, *owns),
            [shape(block, F32), shape(rest, F32), shape(block, BF16), shape(rest, BF16)],
            [pltpu.VMEM((round_up(time_rows + tall, 8), time_width), F32)],
        )
        sent = on_device(fold_body, (other, swap(core_sent, "row", 1)), [shape(rest, BF16)])[0]
        came = [swap(sent_own, "row", 1), swap(sent, "row", bits[1])]
    x2, g1, held = on_device(
        time_body,
        (near, near_cot, far, *centre),
        [shape(y1.shape, BF16)] * 2 + [shape((2 * ch, 2 * cols), BF16)],
    )
    slots = {k: (v,) for k, v in gather(held, "row", bits[1:]).items()}
    slots[1] = (swap(held, "row", 1),)
    for k in list(slots):
        if k > 1:
            halves = (slots[k][0][:ch], slots[k][0][ch:])
            slots[k ^ 1] = tuple(swap(v, "row", 1) for v in halves)
    gathered = [v for k in slot_order(peers) for v in slots[k]]
    count = len(gathered)

    if even:
        rows = space_rows // devices
        period, layout = segments(width)
        full = -(-rows // period) * len(layout)
        deep = round_up(time_rows // devices + full, 16)
        piece = (deep, LANES)
        scratch = (round_up(space_rows + 8 * period + rows, 8), LANES)
        pieces = on_device(
            functools.partial(space_sum_body, count, groups, rows, time_rows // devices),
            gathered,
            [shape((steps, *piece), F32)],
            [pltpu.VMEM((peers, 2 * ch, 2 * cols), BF16)] + [pltpu.VMEM(scratch, F32)] * 2,
        )
        mine, *sends = on_device(
            functools.partial(join_body, time_rows // devices, outer),
            (*pieces, kept, *came),
            [shape(piece, F32)] + [shape(piece, BF16)] * (steps - 1),
        )
        order = sorted(range(1, steps), key=lambda k: (k < steps // 2, k >= steps // 2 and k & 1, -k))
        arrived = [swap(sends[k - 1], "tm", k) for k in order]
        space_share, time_share = on_device(
            functools.partial(final_body, factor, len(layout)),
            (mine, *arrived),
            [shape((full, LANES), F32), shape((time_rows // devices, time_width), F32)],
        )
        space_share = space_share.reshape(-1)[: rows * width]
        time_share = time_share.reshape(-1)
    else:
        total = on_device(
            time_sum_whole_body, (near_cot, far, packed), [shape((time_rows, time_width), F32)]
        )[0]
        time_share = factor * lax.psum_scatter(
            total.reshape(-1), ("tm", "row"), scatter_dimension=0, tiled=True
        )
        total = on_device(
            functools.partial(space_sum_whole_body, count, groups),
            gathered,
            [shape((space_rows, width), F32)],
            [pltpu.VMEM((peers, 2 * ch, 2 * cols), BF16)],
        )[0]
        total = total.reshape(steps, peers, -1)
        total = lax.dynamic_index_in_dim(total, lax.axis_index("row"), 1, keepdims=False)
        space_share = factor * lax.psum_scatter(
            total.reshape(-1), "tm", scatter_dimension=0, tiled=True
        )

    x1, x2, g1, g2 = on_device(
        functools.partial(space_body, count),
        (*gathered, y1, c2, x2, g1, weight_space),
        [shape(y1.shape, BF16)] * 4,
        [pltpu.VMEM((peers + 2, 2 * ch, 2 * cols), BF16)],
    )
    return x1, x2, g1, g2, space_share, time_share


def solution(mesh):
    video = P("tm", "row", None, None)
    share = P(("tm", "row"))
    return jax.shard_map(
        per_device,
        mesh=mesh,
        in_specs=(video,) * 4 + (P(), P()),
        out_specs=(video,) * 4 + (share, share),
        check_vma=False,
    )
```

```python
import functools
import math

import jax
import jax.numpy as jnp
from jax import lax
from jax.experimental import pallas as pl
from jax.experimental.pallas import tpu as pltpu
from jax.sharding import PartitionSpec as P

HAAR = 0.7071067811865476
LANES = 128
F32 = jnp.float32
BF16 = jnp.bfloat16


def round_up(value, unit):
    return (value + unit - 1) // unit * unit


def on_device(body, args, outs, scratch=(), far=0):
    whole = pl.BlockSpec(memory_space=pltpu.VMEM)
    moved = sum(math.prod(a.shape) * a.dtype.itemsize for a in (*args, *outs))
    scratch = [*scratch, *(pltpu.VMEM(a.shape, a.dtype) for a in args[:far])]
    if far:
        scratch.append(pltpu.SemaphoreType.DMA((far,)))
    return pl.pallas_call(
        body,
        out_shape=outs,
        in_specs=[pl.BlockSpec(memory_space=pltpu.HBM)] * far + [whole] * (len(args) - far),
        out_specs=[whole] * len(outs),
        scratch_shapes=scratch,
        compiler_params=pltpu.CompilerParams(vmem_limit_bytes=40 * 1024 * 1024),
        cost_estimate=pl.CostEstimate(flops=0, bytes_accessed=moved, transcendentals=0),
    )(*[pltpu.with_memory_space_constraint(a, pltpu.HBM) for a in args[:far]], *args[far:])


def shape(dims, dtype):
    return jax.ShapeDtypeStruct(tuple(dims), dtype)


def sigmoid(v):
    return 1.0 / (1.0 + jnp.exp(-v))


def silu_slope(v):
    s = sigmoid(v)
    return s * (1.0 + v * (1.0 - s))


def dot(left, right, left_dim, right_dim):
    return lax.dot_general(
        left, right, (((left_dim,), (right_dim,)), ((), ())), preferred_element_type=F32
    )


def squeezed(ref):
    even, odd = ref[0, 0].astype(F32), ref[1, 0].astype(F32)
    return jnp.concatenate([(even + odd) * HAAR, (even - odd) * HAAR], axis=-1)


def unsqueezed(packed):
    half = packed.shape[-1] // 2
    low, high = packed[:, :half], packed[:, half:]
    return (low + high) * HAAR, (low - high) * HAAR


def fetch(far, near, sems):
    copies = [pltpu.make_async_copy(f, n, sems.at[i]) for i, (f, n) in enumerate(zip(far, near))]
    for copy in copies:
        copy.start()
    for copy in copies:
        copy.wait()


def open_body(y_far, cot_far, out_ref, y_ref, cot_ref, sems):
    fetch((y_far, cot_far), (y_ref, cot_ref), sems)
    sq = squeezed(y_ref)
    cols = sq.shape[0]
    out_ref[:cols] = (sq * sigmoid(sq)).astype(BF16)
    out_ref[cols:] = squeezed(cot_ref).astype(BF16)


def centre_body(y1_far, y2_far, c1_far, weight_far, own, *refs):
    (forth, back, slope, base, weight_out), (y1, y2, c1, weight, sems) = refs[:5], refs[5:]
    fetch((y1_far, y2_far, c1_far, weight_far), (y1, y2, c1, weight), sems)
    cols = own.shape[0] // 2
    groups, width = weight.shape[1:3]
    for q in range(groups):
        lanes = slice(q * width, (q + 1) * width)
        forth[:, lanes] = dot(own[:cols, lanes], weight[1, q], 1, 0)
        back[:, lanes] = dot(own[cols:, lanes], weight[1, q], 1, 1)
    slope[...] = silu_slope(squeezed(y1))
    for f in range(2):
        base[0, f] = y2[f, 0]
        base[1, f] = c1[f, 0]
    weight_out[...] = weight[...]


def time_body(near, near_cot, far, forth0, back0, slope, base, weight, x2_out, g1_out, held_out):
    cols = forth0.shape[0]
    groups, width = weight.shape[1:3]
    tap = jnp.where(lax.axis_index("tm") % 2 == 0, 2, 0)
    forth, back = [], []
    for q in range(groups):
        lanes = slice(q * width, (q + 1) * width)
        sides = jnp.concatenate([near[:cols, lanes], far[:cols, lanes]], axis=1)
        taps = jnp.concatenate([weight[tap, q], weight[2 - tap, q]], axis=0)
        forth.append(forth0[:, lanes] + dot(sides, taps, 1, 0))
        sides = jnp.concatenate([near_cot[:, lanes], far[cols:, lanes]], axis=1)
        taps = jnp.concatenate([weight[2 - tap, q], weight[tap, q]], axis=1)
        back.append(back0[:, lanes] + dot(sides, taps, 1, 1))
    branch = unsqueezed(jnp.concatenate(forth, axis=-1))
    back = unsqueezed(jnp.concatenate(back, axis=-1) * slope[...])
    acts, cots = [], []
    for f in range(2):
        x2 = (base[0, f].astype(F32) - branch[f].astype(BF16).astype(F32)).astype(BF16)
        g1 = (base[1, f].astype(F32) + back[f].astype(BF16).astype(F32)).astype(BF16)
        x2_out[f, 0] = x2
        g1_out[f, 0] = g1
        v = x2.astype(F32)
        acts.append(v * sigmoid(v))
        cots.append(g1.astype(F32))
    ch = held_out.shape[0] // 2
    held_out[:ch] = jnp.concatenate(acts, axis=0).astype(BF16).T
    held_out[ch:] = jnp.concatenate(cots, axis=0).astype(BF16).T


def time_terms(near_cot, far, owns, total):
    cols = far.shape[0] // 2
    width = total.shape[1]
    groups = far.shape[1] // width
    act = jnp.concatenate([v[:cols] for v in owns], axis=0).T
    own = jnp.concatenate([v[cols:] for v in owns], axis=0)
    tap = jnp.where(lax.axis_index("tm") % 2 == 0, 0, 2)
    for k, cot in ((1, own), (tap, near_cot[...]), (2 - tap, far[cols:])):
        for q in range(groups):
            part = slice(q * width, (q + 1) * width)
            at = pl.multiple_of((k * groups + q) * width, width)
            total[pl.ds(at, width), :] = dot(act[part, : cot.shape[0]], cot[:, part], 1, 0)


def outer_steps(steps, peers, taps, rows):
    size = steps * peers * rows // taps
    return [
        t
        for t in range(steps)
        if t * peers * rows < size or (t + 1) * peers * rows > (taps - 1) * size
    ]


def time_sum_body(offsets, rows, near_cot, far, *refs):
    owns, refs, total = refs[: len(offsets)], refs[len(offsets) : -1], refs[-1]
    keeps, sends = refs[: len(offsets)], refs[len(offsets) :]
    time_terms(near_cot, far, owns, total)
    me, peers, steps = lax.axis_index("row"), lax.axis_size("row"), lax.axis_size("tm")
    held, third = keeps[0].shape[1], steps * peers * rows // 3
    for u, offset in enumerate(offsets):
        if u == 1:
            total[third : 2 * third] = jnp.zeros((third, total.shape[1]), F32)
        for i, t in enumerate(range(steps) if u == 0 else outer_steps(steps, peers, 3, rows)):
            mine = (t * peers + (me ^ offset)) * rows
            other = (t * peers + (me ^ offset ^ 1)) * rows
            keeps[u][i] = total[pl.ds(mine, held), :]
            sends[u][i] = total[pl.ds(other, held), :].astype(BF16)


def time_sum_whole_body(near_cot, far, own, total):
    time_terms(near_cot, far, (own,), total)


def fold_body(kept, came, send):
    send[...] = (kept[...] + came[...].astype(F32)).astype(BF16)


def place(slots, rows_ref, lead):
    me, ch = lax.axis_index("row"), rows_ref.shape[1]
    peers = lax.axis_size("row")
    whole = peers // 2 + 1
    rest = slots[whole:]
    parts = len(rest) // (peers - whole) if rest else 1
    slots = [(v,) for v in slots[:whole]] + [
        rest[i : i + parts] for i in range(0, len(rest), parts)
    ]
    for k, refs in zip(slot_order(peers), slots):
        for j, ref in enumerate(refs):
            size = ch // len(refs)
            rows_ref[(me ^ k) + lead, j * size : (j + 1) * size] = ref[...]


def space_terms(slots, rows_ref, cols, store):
    peers = lax.axis_size("row")
    ch = rows_ref.shape[1] // 2
    place(slots, rows_ref, 0)
    column = lax.broadcasted_iota(jnp.int32, (ch, LANES), 1) % cols
    act, shifts = [], ([], [], [])
    for r in range(peers):
        act.append(rows_ref[r, :ch])
        cot = rows_ref[r, ch:]
        wide = cot.astype(F32)
        later = jnp.where(column == cols - 1, 0.0, pltpu.roll(wide, LANES - 1, 1))
        sooner = jnp.where(column == 0, 0.0, pltpu.roll(wide, 1, 1))
        for held, value in zip(shifts, (later.astype(BF16), cot, sooner.astype(BF16))):
            held.append(value)
    for a in range(3):
        pairs = [(r, r - a + 1) for r in range(peers) if 0 <= r - a + 1 < peers]
        left = jnp.concatenate([act[r] for r, _ in pairs], axis=1)
        for b in range(3):
            right = jnp.concatenate([shifts[b][r] for _, r in pairs], axis=1)
            store(a * 3 + b, left, right)


def segments(width):
    period = LANES // math.gcd(width, LANES)
    found = []
    for j in range(period * width // LANES):
        row, lane = [], 0
        while lane < LANES:
            at = j * LANES + lane
            source, column = divmod(at, width)
            tile, first = divmod(column, LANES)
            row.append((lane, source, tile, (lane - first) % LANES))
            lane += min(LANES - first, width - column, LANES - lane)
        found.append(row)
    return period, found


def space_sum_body(count, groups, rows, time_rows, *refs):
    peers, steps = lax.axis_size("row"), lax.axis_size("tm")
    slots, refs = refs[:count], refs[count:]
    out, rows_ref, main, rest = refs
    ch = rows_ref.shape[1] // 2
    width = ch // groups

    def store(tap, left, right):
        for q in range(groups):
            part = slice(q * width, (q + 1) * width)
            term = dot(left[part], right[part], 1, 1)
            at = pl.ds((tap * groups + q) * width, width)
            main[at, :] = term[:, :LANES]
            rest[at, : width - LANES] = term[:, LANES:]

    space_terms(slots, rows_ref, LANES // 2, store)
    period, layout = segments(width)
    held = round_up(-(-rows // period), 8)
    lane = lax.broadcasted_iota(jnp.int32, (held, LANES), 1)
    here, me = lax.axis_index("tm"), lax.axis_index("row")
    short = -(-rows // period)
    for k in range(steps):
        t = here ^ k
        start = (t * peers + me) * rows
        rolled = {}

        def source(j, tile, amount):
            if (j, tile, amount) not in rolled:
                ref = (main, rest)[tile]
                value = ref[pl.ds(start + j, held, stride=period), :]
                rolled[j, tile, amount] = pltpu.roll(value, amount, 1) if amount else value
            return rolled[j, tile, amount]

        parts = [jnp.zeros((time_rows, LANES), F32)]
        for row in layout:
            value = None
            for first, j, tile, amount in row:
                piece = source(j, tile, amount)
                value = piece if value is None else jnp.where(lane < first, value, piece)
            parts.append(value[:short])
        blank = out.shape[1] - time_rows - short * len(layout)
        if blank:
            parts.append(jnp.zeros((blank, LANES), F32))
        out[k] = jnp.concatenate(parts, axis=0)


def join_body(time_rows, outer, pieces, kept, core_came, came, mine, *sends):
    tall, steps = kept.shape[1], kept.shape[0]
    row = lax.broadcasted_iota(jnp.int32, (tall, LANES), 0)
    gap = steps - len(outer)
    for k in range(pieces.shape[0]):
        t = lax.axis_index("tm") ^ k
        first = next((i for i, v in enumerate(outer) if v != i), len(outer))
        over = t >= first + gap
        sent = jnp.logical_or(t < first, over)
        terms = came[jnp.where(over, t - gap, jnp.minimum(t, len(outer) - 1))].astype(F32)
        terms = kept[t] + core_came[t].astype(F32) + jnp.where(sent, terms, 0.0)
        head = pieces[k, :tall] + jnp.where(row < time_rows, terms, 0.0)
        piece = jnp.concatenate([head, pieces[k, tall:]], axis=0)
        if k == 0:
            mine[...] = piece
        else:
            sends[k - 1][...] = piece.astype(BF16)


def space_sum_whole_body(count, groups, *refs):
    slots, (total, rows_ref) = refs[:count], refs[count:]
    ch = rows_ref.shape[1] // 2
    width = ch // groups

    def store(tap, left, right):
        for q in range(groups):
            part = slice(q * width, (q + 1) * width)
            at = pl.ds((tap * groups + q) * width, width)
            total[at, :] = dot(left[part], right[part], 1, 1)

    space_terms(slots, rows_ref, LANES // 2, store)


def final_body(factor, stride, short, *refs):
    (mine, *came), (space_out, time_out) = refs[:-2], refs[-2:]
    total = mine[...]
    for ref in came:
        total = total + ref[...].astype(F32)
    total = total * factor
    first, held = time_out.shape[0], space_out.shape[0] // stride
    time_out[...] = total[:first]
    for j in range(stride):
        at = first + j * short
        space_out[pl.ds(j, held, stride=stride), :] = total[at : at + held]


def space_body(count, *refs):
    peers = lax.axis_size("row")
    slots, refs = refs[:count], refs[count:]
    y1, c2, x2, g1, weight, x1_out, x2_out, g1_out, g2_out, rows_ref = refs
    x2_out[...] = x2[...]
    g1_out[...] = g1[...]
    me = lax.axis_index("row")
    cols, ch = y1.shape[2:]
    groups, width = weight.shape[2:4]
    rows_ref[0] = jnp.zeros(rows_ref.shape[1:], BF16)
    rows_ref[peers + 1] = jnp.zeros(rows_ref.shape[1:], BF16)
    place(slots, rows_ref, 1)
    column = lax.broadcasted_iota(jnp.int32, (LANES, width), 0) % cols
    forth, back = [None] * groups, [None] * groups
    for a in range(3):
        row = rows_ref[me + a].astype(F32).T
        for q in range(groups):
            for first, sums in ((0, forth), (ch, back)):
                value = row[:, first + q * width : first + (q + 1) * width]
                sooner = jnp.where(column == 0, 0.0, pltpu.roll(value, 1, 0))
                later = jnp.where(column == cols - 1, 0.0, pltpu.roll(value, LANES - 1, 0))
                for b, moved in enumerate((sooner, value, later)):
                    if first:
                        term = dot(moved.astype(BF16), weight[2 - a, 2 - b, q], 1, 1)
                    else:
                        term = dot(moved.astype(BF16), weight[a, b, q], 1, 0)
                    sums[q] = term if sums[q] is None else sums[q] + term
    forth = jnp.concatenate(forth, axis=-1)
    back = jnp.concatenate(back, axis=-1)
    for f in range(2):
        part = slice(f * cols, (f + 1) * cols)
        x1_out[f, 0] = (y1[f, 0].astype(F32) - forth[part]).astype(BF16)
        slope = silu_slope(x2[f, 0].astype(F32))
        g2_out[f, 0] = (c2[f, 0].astype(F32) + slope * back[part]).astype(BF16)


def swap(x, axis, bit):
    return lax.ppermute(x, axis, [(i, i ^ bit) for i in range(lax.axis_size(axis))])


def gather(x, axis, bits):
    slots = {0: x}
    for bit in reversed(bits):
        for k in list(slots):
            slots[k ^ bit] = swap(slots[k], axis, bit)
    return slots


def slot_order(peers):
    last = [k for k in range(peers) if k & 1 and k > 1]
    return [k for k in range(peers) if k not in last] + last


def row_offsets(bits):
    if not bits:
        return [0]
    rest = row_offsets(bits[1:])
    return rest + [o ^ bits[0] for o in rest]


def neighbours(x, axis, first):
    lower = range(first, lax.axis_size(axis) - 1, 2)
    return lax.ppermute(x, axis, [p for i in lower for p in ((i, i + 1), (i + 1, i))])


def per_device(y1, y2, c1, c2, weight_space, temporal_weight):
    steps, peers = lax.axis_size("tm"), lax.axis_size("row")
    devices = steps * peers
    frames, rows_here, cols, ch = y1.shape
    groups = weight_space.shape[2]
    width = ch // groups
    taps = weight_space.shape[0] * weight_space.shape[1]
    factor = 1.0 / math.sqrt(frames * rows_here * cols * devices)
    time_groups, time_width = temporal_weight.shape[1:3]
    time_rows = 3 * time_groups * time_width
    space_rows = taps * ch

    packed = on_device(open_body, (y1, c2), [shape((2 * cols, 2 * ch), BF16)], far=2)[0]
    up = [(i, i + 1) for i in range(steps - 1)]
    near, far = neighbours(packed, "tm", 0), neighbours(packed, "tm", 1)
    wide = shape((cols, 2 * ch), F32)
    centre = on_device(
        centre_body,
        (y1, y2, c1, temporal_weight, packed),
        [wide] * 3 + [shape((2, 2, cols, ch), BF16), shape(temporal_weight.shape, BF16)],
        far=4,
    )

    near, centre = lax.optimization_barrier((near, centre))
    near_cot = near[cols:]
    bits = [1 << i for i in range(peers.bit_length() - 1)]
    even = time_rows % devices == 0 and space_rows % devices == 0 and peers == 4
    owns = gather(packed, "row", bits[1:]) if even else {0: packed}
    owns = [owns[k] for k in sorted(owns)]
    if even:
        rows = time_rows // devices
        tall = round_up(rows, 16)
        offsets = row_offsets(bits[1:])
        block = (steps, tall, time_width)
        outer = outer_steps(steps, peers, 3, rows)
        rest = (len(outer), *block[1:])
        kept, other, sent_own, core_sent = on_device(
            functools.partial(time_sum_body, offsets, rows),
            (near_cot, far, *owns),
            [shape(block, F32), shape(rest, F32), shape(block, BF16), shape(rest, BF16)],
            [pltpu.VMEM((round_up(time_rows + tall, 8), time_width), F32)],
        )
        sent = on_device(fold_body, (other, swap(core_sent, "row", 1)), [shape(rest, BF16)])[0]
        came = [swap(sent_own, "row", 1), swap(sent, "row", bits[1])]
    x2, g1, held = on_device(
        time_body,
        (near, near_cot, far, *centre),
        [shape(y1.shape, BF16)] * 2 + [shape((2 * ch, 2 * cols), BF16)],
    )
    slots = {k: (v,) for k, v in gather(held, "row", bits[1:]).items()}
    slots[1] = (swap(held, "row", 1),)
    for k in list(slots):
        if k > 1:
            halves = (slots[k][0][:ch], slots[k][0][ch:])
            slots[k ^ 1] = tuple(swap(v, "row", 1) for v in halves)
    gathered = [v for k in slot_order(peers) for v in slots[k]]
    count = len(gathered)

    if even:
        rows = space_rows // devices
        period, layout = segments(width)
        short = -(-rows // period)
        held_rows = round_up(short, 8)
        full = short * len(layout)
        deep = round_up(time_rows // devices + full - short + held_rows, 16)
        piece = (deep, LANES)
        scratch = (round_up(space_rows + 8 * period + rows, 8), LANES)
        pieces = on_device(
            functools.partial(space_sum_body, count, groups, rows, time_rows // devices),
            gathered,
            [shape((steps, *piece), F32)],
            [pltpu.VMEM((peers, 2 * ch, 2 * cols), BF16)] + [pltpu.VMEM(scratch, F32)] * 2,
        )
        mine, *sends = on_device(
            functools.partial(join_body, time_rows // devices, outer),
            (*pieces, kept, *came),
            [shape(piece, F32)] + [shape(piece, BF16)] * (steps - 1),
        )
        order = sorted(range(1, steps), key=lambda k: (k < steps // 2, k >= steps // 2 and k & 1, -k))
        arrived = [swap(sends[k - 1], "tm", k) for k in order]
        space_share, time_share = on_device(
            functools.partial(final_body, factor, len(layout), short),
            (mine, *arrived),
            [
                shape((held_rows * len(layout), LANES), F32),
                shape((time_rows // devices, time_width), F32),
            ],
        )
        space_share = space_share.reshape(-1)[: rows * width]
        time_share = time_share.reshape(-1)
    else:
        total = on_device(
            time_sum_whole_body, (near_cot, far, packed), [shape((time_rows, time_width), F32)]
        )[0]
        time_share = factor * lax.psum_scatter(
            total.reshape(-1), ("tm", "row"), scatter_dimension=0, tiled=True
        )
        total = on_device(
            functools.partial(space_sum_whole_body, count, groups),
            gathered,
            [shape((space_rows, width), F32)],
            [pltpu.VMEM((peers, 2 * ch, 2 * cols), BF16)],
        )[0]
        total = total.reshape(steps, peers, -1)
        total = lax.dynamic_index_in_dim(total, lax.axis_index("row"), 1, keepdims=False)
        space_share = factor * lax.psum_scatter(
            total.reshape(-1), "tm", scatter_dimension=0, tiled=True
        )

    x1, x2, g1, g2 = on_device(
        functools.partial(space_body, count),
        (*gathered, y1, c2, x2, g1, weight_space),
        [shape(y1.shape, BF16)] * 4,
        [pltpu.VMEM((peers + 2, 2 * ch, 2 * cols), BF16)],
    )
    return x1, x2, g1, g2, space_share, time_share


def solution(mesh):
    video = P("tm", "row", None, None)
    share = P(("tm", "row"))
    return jax.shard_map(
        per_device,
        mesh=mesh,
        in_specs=(video,) * 4 + (P(), P()),
        out_specs=(video,) * 4 + (share, share),
        check_vma=False,
    )
```

```python
import functools
import math

import jax
import jax.numpy as jnp
from jax import lax
from jax.experimental import pallas as pl
from jax.experimental.pallas import tpu as pltpu
from jax.sharding import PartitionSpec as P

HAAR = 0.7071067811865476
LANES = 128
F32 = jnp.float32
BF16 = jnp.bfloat16


def round_up(value, unit):
    return (value + unit - 1) // unit * unit


def on_device(body, args, outs, scratch=(), far=0):
    whole = pl.BlockSpec(memory_space=pltpu.VMEM)
    moved = sum(math.prod(a.shape) * a.dtype.itemsize for a in (*args, *outs))
    scratch = [*scratch, *(pltpu.VMEM(a.shape, a.dtype) for a in args[:far])]
    if far:
        scratch.append(pltpu.SemaphoreType.DMA((far,)))
    return pl.pallas_call(
        body,
        out_shape=outs,
        in_specs=[pl.BlockSpec(memory_space=pltpu.HBM)] * far + [whole] * (len(args) - far),
        out_specs=[whole] * len(outs),
        scratch_shapes=scratch,
        compiler_params=pltpu.CompilerParams(vmem_limit_bytes=40 * 1024 * 1024),
        cost_estimate=pl.CostEstimate(flops=0, bytes_accessed=moved, transcendentals=0),
    )(*[pltpu.with_memory_space_constraint(a, pltpu.HBM) for a in args[:far]], *args[far:])


def shape(dims, dtype):
    return jax.ShapeDtypeStruct(tuple(dims), dtype)


def sigmoid(v):
    return 1.0 / (1.0 + jnp.exp(-v))


def silu_slope(v):
    s = sigmoid(v)
    return s * (1.0 + v * (1.0 - s))


def dot(left, right, left_dim, right_dim):
    return lax.dot_general(
        left, right, (((left_dim,), (right_dim,)), ((), ())), preferred_element_type=F32
    )


def squeezed(ref):
    even, odd = ref[0, 0].astype(F32), ref[1, 0].astype(F32)
    return jnp.concatenate([(even + odd) * HAAR, (even - odd) * HAAR], axis=-1)


def unsqueezed(packed):
    half = packed.shape[-1] // 2
    low, high = packed[:, :half], packed[:, half:]
    return (low + high) * HAAR, (low - high) * HAAR


def fetch(far, near, sems):
    copies = [pltpu.make_async_copy(f, n, sems.at[i]) for i, (f, n) in enumerate(zip(far, near))]
    for copy in copies:
        copy.start()
    for copy in copies:
        copy.wait()


def open_body(y_far, cot_far, out_ref, y_ref, cot_ref, sems):
    fetch((y_far, cot_far), (y_ref, cot_ref), sems)
    sq = squeezed(y_ref)
    cols = sq.shape[0]
    out_ref[:cols] = (sq * sigmoid(sq)).astype(BF16)
    out_ref[cols:] = squeezed(cot_ref).astype(BF16)


def centre_body(y1_far, y2_far, c1_far, weight_far, own, *refs):
    (forth, back, slope, base, weight_out), (y1, y2, c1, weight, sems) = refs[:5], refs[5:]
    fetch((y1_far, y2_far, c1_far, weight_far), (y1, y2, c1, weight), sems)
    cols = own.shape[0] // 2
    groups, width = weight.shape[1:3]
    for q in range(groups):
        lanes = slice(q * width, (q + 1) * width)
        forth[:, lanes] = dot(own[:cols, lanes], weight[1, q], 1, 0)
        back[:, lanes] = dot(own[cols:, lanes], weight[1, q], 1, 1)
    slope[...] = silu_slope(squeezed(y1))
    for f in range(2):
        base[0, f] = y2[f, 0]
        base[1, f] = c1[f, 0]
    weight_out[...] = weight[...]


def time_body(near, near_cot, far, forth0, back0, slope, base, weight, x2_out, g1_out, held_out):
    cols = forth0.shape[0]
    groups, width = weight.shape[1:3]
    tap = jnp.where(lax.axis_index("tm") % 2 == 0, 2, 0)
    forth, back = [], []
    for q in range(groups):
        lanes = slice(q * width, (q + 1) * width)
        sides = jnp.concatenate([near[:cols, lanes], far[:cols, lanes]], axis=1)
        taps = jnp.concatenate([weight[tap, q], weight[2 - tap, q]], axis=0)
        forth.append(forth0[:, lanes] + dot(sides, taps, 1, 0))
        sides = jnp.concatenate([near_cot[:, lanes], far[cols:, lanes]], axis=1)
        taps = jnp.concatenate([weight[2 - tap, q], weight[tap, q]], axis=1)
        back.append(back0[:, lanes] + dot(sides, taps, 1, 1))
    branch = unsqueezed(jnp.concatenate(forth, axis=-1))
    back = unsqueezed(jnp.concatenate(back, axis=-1) * slope[...])
    acts, cots = [], []
    for f in range(2):
        x2 = (base[0, f].astype(F32) - branch[f].astype(BF16).astype(F32)).astype(BF16)
        g1 = (base[1, f].astype(F32) + back[f].astype(BF16).astype(F32)).astype(BF16)
        x2_out[f, 0] = x2
        g1_out[f, 0] = g1
        v = x2.astype(F32)
        acts.append(v * sigmoid(v))
        cots.append(g1.astype(F32))
    ch = held_out.shape[0] // 2
    held_out[:ch] = jnp.concatenate(acts, axis=0).astype(BF16).T
    held_out[ch:] = jnp.concatenate(cots, axis=0).astype(BF16).T


def time_terms(acts, pairs, total):
    width = total.shape[1]
    act = jnp.concatenate(acts, axis=0).T
    groups = act.shape[0] // width
    for k, cot in pairs:
        for q in range(groups):
            part = slice(q * width, (q + 1) * width)
            at = pl.multiple_of((k * groups + q) * width, width)
            total[pl.ds(at, width), :] = dot(act[part], cot[:, part], 1, 0)


def side_terms(near_cot, far, own, total):
    cols = far.shape[0] // 2
    tap = jnp.where(lax.axis_index("tm") % 2 == 0, 0, 2)
    time_terms([own[:cols]], ((tap, near_cot[...]), (2 - tap, far[cols:])), total)


def middle_terms(owns, total):
    cols = owns[0].shape[0] // 2
    cot = jnp.concatenate([v[cols:] for v in owns], axis=0)
    time_terms([v[:cols] for v in owns], ((1, cot),), total)


def outer_steps(steps, peers, taps, rows):
    size = steps * peers * rows // taps
    return [
        t
        for t in range(steps)
        if t * peers * rows < size or (t + 1) * peers * rows > (taps - 1) * size
    ]


def time_outer_body(rows, offset, near_cot, far, own, keep, send, total):
    me, peers, steps = lax.axis_index("row"), lax.axis_size("row"), lax.axis_size("tm")
    held, third = keep.shape[1], steps * peers * rows // 3
    total[third : 2 * third] = jnp.zeros((third, total.shape[1]), F32)
    side_terms(near_cot, far, own, total)
    for i, t in enumerate(outer_steps(steps, peers, 3, rows)):
        mine = (t * peers + (me ^ offset)) * rows
        other = (t * peers + (me ^ offset ^ 1)) * rows
        keep[i] = total[pl.ds(mine, held), :]
        send[i] = total[pl.ds(other, held), :].astype(BF16)


def time_own_body(rows, outer, *refs):
    owns, (keep, send, total) = refs[:-3], refs[-3:]
    me, peers, steps = lax.axis_index("row"), lax.axis_size("row"), lax.axis_size("tm")
    held, third = keep.shape[1], steps * peers * rows // 3
    total[:third] = outer[:third]
    total[2 * third :] = outer[2 * third :]
    middle_terms(owns, total)
    for t in range(steps):
        keep[t] = total[pl.ds((t * peers + me) * rows, held), :]
        send[t] = total[pl.ds((t * peers + (me ^ 1)) * rows, held), :].astype(BF16)


def time_sum_whole_body(near_cot, far, own, total):
    side_terms(near_cot, far, own, total)
    middle_terms((own,), total)


def fold_body(kept, came, send):
    send[...] = (kept[...] + came[...].astype(F32)).astype(BF16)


def place(slots, rows_ref, lead):
    me, ch = lax.axis_index("row"), rows_ref.shape[1]
    peers = lax.axis_size("row")
    whole = peers // 2 + 1
    rest = slots[whole:]
    parts = len(rest) // (peers - whole) if rest else 1
    slots = [(v,) for v in slots[:whole]] + [
        rest[i : i + parts] for i in range(0, len(rest), parts)
    ]
    for k, refs in zip(slot_order(peers), slots):
        for j, ref in enumerate(refs):
            size = ch // len(refs)
            rows_ref[(me ^ k) + lead, j * size : (j + 1) * size] = ref[...]


def space_terms(slots, rows_ref, cols, store):
    peers = lax.axis_size("row")
    ch = rows_ref.shape[1] // 2
    place(slots, rows_ref, 0)
    column = lax.broadcasted_iota(jnp.int32, (ch, LANES), 1) % cols
    act, shifts = [], ([], [], [])
    for r in range(peers):
        act.append(rows_ref[r, :ch])
        cot = rows_ref[r, ch:]
        wide = cot.astype(F32)
        later = jnp.where(column == cols - 1, 0.0, pltpu.roll(wide, LANES - 1, 1))
        sooner = jnp.where(column == 0, 0.0, pltpu.roll(wide, 1, 1))
        for held, value in zip(shifts, (later.astype(BF16), cot, sooner.astype(BF16))):
            held.append(value)
    for a in range(3):
        pairs = [(r, r - a + 1) for r in range(peers) if 0 <= r - a + 1 < peers]
        left = jnp.concatenate([act[r] for r, _ in pairs], axis=1)
        for b in range(3):
            right = jnp.concatenate([shifts[b][r] for _, r in pairs], axis=1)
            store(a * 3 + b, left, right)


def segments(width):
    period = LANES // math.gcd(width, LANES)
    found = []
    for j in range(period * width // LANES):
        row, lane = [], 0
        while lane < LANES:
            at = j * LANES + lane
            source, column = divmod(at, width)
            tile, first = divmod(column, LANES)
            row.append((lane, source, tile, (lane - first) % LANES))
            lane += min(LANES - first, width - column, LANES - lane)
        found.append(row)
    return period, found


def space_sum_body(count, groups, rows, time_rows, *refs):
    peers, steps = lax.axis_size("row"), lax.axis_size("tm")
    slots, refs = refs[:count], refs[count:]
    out, rows_ref, main, rest = refs
    ch = rows_ref.shape[1] // 2
    width = ch // groups

    def store(tap, left, right):
        for q in range(groups):
            part = slice(q * width, (q + 1) * width)
            term = dot(left[part], right[part], 1, 1)
            at = pl.ds((tap * groups + q) * width, width)
            main[at, :] = term[:, :LANES]
            rest[at, : width - LANES] = term[:, LANES:]

    space_terms(slots, rows_ref, LANES // 2, store)
    period, layout = segments(width)
    held = round_up(-(-rows // period), 8)
    lane = lax.broadcasted_iota(jnp.int32, (held, LANES), 1)
    here, me = lax.axis_index("tm"), lax.axis_index("row")
    short = -(-rows // period)
    for k in range(steps):
        t = here ^ k
        start = (t * peers + me) * rows
        rolled = {}

        def source(j, tile, amount):
            if (j, tile, amount) not in rolled:
                ref = (main, rest)[tile]
                value = ref[pl.ds(start + j, held, stride=period), :]
                rolled[j, tile, amount] = pltpu.roll(value, amount, 1) if amount else value
            return rolled[j, tile, amount]

        parts = [jnp.zeros((time_rows, LANES), F32)]
        for row in layout:
            value = None
            for first, j, tile, amount in row:
                piece = source(j, tile, amount)
                value = piece if value is None else jnp.where(lane < first, value, piece)
            parts.append(value[:short])
        blank = out.shape[1] - time_rows - short * len(layout)
        if blank:
            parts.append(jnp.zeros((blank, LANES), F32))
        out[k] = jnp.concatenate(parts, axis=0)


def join_body(time_rows, outer, pieces, kept, core_came, came, mine, *sends):
    tall, steps = kept.shape[1], kept.shape[0]
    row = lax.broadcasted_iota(jnp.int32, (tall, LANES), 0)
    gap = steps - len(outer)
    for k in range(pieces.shape[0]):
        t = lax.axis_index("tm") ^ k
        first = next((i for i, v in enumerate(outer) if v != i), len(outer))
        over = t >= first + gap
        sent = jnp.logical_or(t < first, over)
        terms = came[jnp.where(over, t - gap, jnp.minimum(t, len(outer) - 1))].astype(F32)
        terms = kept[t] + core_came[t].astype(F32) + jnp.where(sent, terms, 0.0)
        head = pieces[k, :tall] + jnp.where(row < time_rows, terms, 0.0)
        piece = jnp.concatenate([head, pieces[k, tall:]], axis=0)
        if k == 0:
            mine[...] = piece
        else:
            sends[k - 1][...] = piece.astype(BF16)


def space_sum_whole_body(count, groups, *refs):
    slots, (total, rows_ref) = refs[:count], refs[count:]
    ch = rows_ref.shape[1] // 2
    width = ch // groups

    def store(tap, left, right):
        for q in range(groups):
            part = slice(q * width, (q + 1) * width)
            at = pl.ds((tap * groups + q) * width, width)
            total[at, :] = dot(left[part], right[part], 1, 1)

    space_terms(slots, rows_ref, LANES // 2, store)


def final_body(factor, stride, short, *refs):
    (mine, *came), (space_out, time_out) = refs[:-2], refs[-2:]
    total = mine[...]
    for ref in came:
        total = total + ref[...].astype(F32)
    total = total * factor
    first, held = time_out.shape[0], space_out.shape[0] // stride
    time_out[...] = total[:first]
    for j in range(stride):
        at = first + j * short
        space_out[pl.ds(j, held, stride=stride), :] = total[at : at + held]


def space_body(count, *refs):
    peers = lax.axis_size("row")
    slots, refs = refs[:count], refs[count:]
    y1, c2, x2, g1, weight, x1_out, x2_out, g1_out, g2_out, rows_ref = refs
    x2_out[...] = x2[...]
    g1_out[...] = g1[...]
    me = lax.axis_index("row")
    cols, ch = y1.shape[2:]
    groups, width = weight.shape[2:4]
    rows_ref[0] = jnp.zeros(rows_ref.shape[1:], BF16)
    rows_ref[peers + 1] = jnp.zeros(rows_ref.shape[1:], BF16)
    place(slots, rows_ref, 1)
    column = lax.broadcasted_iota(jnp.int32, (LANES, width), 0) % cols
    forth, back = [None] * groups, [None] * groups
    for a in range(3):
        row = rows_ref[me + a].astype(F32).T
        for q in range(groups):
            for first, sums in ((0, forth), (ch, back)):
                value = row[:, first + q * width : first + (q + 1) * width]
                sooner = jnp.where(column == 0, 0.0, pltpu.roll(value, 1, 0))
                later = jnp.where(column == cols - 1, 0.0, pltpu.roll(value, LANES - 1, 0))
                for b, moved in enumerate((sooner, value, later)):
                    if first:
                        term = dot(moved.astype(BF16), weight[2 - a, 2 - b, q], 1, 1)
                    else:
                        term = dot(moved.astype(BF16), weight[a, b, q], 1, 0)
                    sums[q] = term if sums[q] is None else sums[q] + term
    forth = jnp.concatenate(forth, axis=-1)
    back = jnp.concatenate(back, axis=-1)
    for f in range(2):
        part = slice(f * cols, (f + 1) * cols)
        x1_out[f, 0] = (y1[f, 0].astype(F32) - forth[part]).astype(BF16)
        slope = silu_slope(x2[f, 0].astype(F32))
        g2_out[f, 0] = (c2[f, 0].astype(F32) + slope * back[part]).astype(BF16)


def swap(x, axis, bit):
    return lax.ppermute(x, axis, [(i, i ^ bit) for i in range(lax.axis_size(axis))])


def gather(x, axis, bits):
    slots = {0: x}
    for bit in reversed(bits):
        for k in list(slots):
            slots[k ^ bit] = swap(slots[k], axis, bit)
    return slots


def slot_order(peers):
    last = [k for k in range(peers) if k & 1 and k > 1]
    return [k for k in range(peers) if k not in last] + last


def row_offsets(bits):
    if not bits:
        return [0]
    rest = row_offsets(bits[1:])
    return rest + [o ^ bits[0] for o in rest]


def neighbours(x, axis, first):
    lower = range(first, lax.axis_size(axis) - 1, 2)
    return lax.ppermute(x, axis, [p for i in lower for p in ((i, i + 1), (i + 1, i))])


def per_device(y1, y2, c1, c2, weight_space, temporal_weight):
    steps, peers = lax.axis_size("tm"), lax.axis_size("row")
    devices = steps * peers
    frames, rows_here, cols, ch = y1.shape
    groups = weight_space.shape[2]
    width = ch // groups
    taps = weight_space.shape[0] * weight_space.shape[1]
    factor = 1.0 / math.sqrt(frames * rows_here * cols * devices)
    time_groups, time_width = temporal_weight.shape[1:3]
    time_rows = 3 * time_groups * time_width
    space_rows = taps * ch

    packed = on_device(open_body, (y1, c2), [shape((2 * cols, 2 * ch), BF16)], far=2)[0]
    up = [(i, i + 1) for i in range(steps - 1)]
    near, far = neighbours(packed, "tm", 0), neighbours(packed, "tm", 1)
    wide = shape((cols, 2 * ch), F32)
    centre = on_device(
        centre_body,
        (y1, y2, c1, temporal_weight, packed),
        [wide] * 3 + [shape((2, 2, cols, ch), BF16), shape(temporal_weight.shape, BF16)],
        far=4,
    )

    near, centre = lax.optimization_barrier((near, centre))
    near_cot = near[cols:]
    bits = [1 << i for i in range(peers.bit_length() - 1)]
    even = time_rows % devices == 0 and space_rows % devices == 0 and peers == 4
    owns = gather(packed, "row", bits[1:]) if even else {0: packed}
    owns = [owns[k] for k in sorted(owns)]
    if even:
        rows = time_rows // devices
        tall = round_up(rows, 16)
        offsets = row_offsets(bits[1:])
        block = (steps, tall, time_width)
        outer = outer_steps(steps, peers, 3, rows)
        rest = (len(outer), *block[1:])
        table = shape((round_up(time_rows + tall, 8), time_width), F32)
        other, core_sent, table_outer = on_device(
            functools.partial(time_outer_body, rows, offsets[1]),
            (near_cot, far, packed),
            [shape(rest, F32), shape(rest, BF16), table],
        )
        kept, sent_own = on_device(
            functools.partial(time_own_body, rows),
            (table_outer, *owns),
            [shape(block, F32), shape(block, BF16)],
            [pltpu.VMEM(table.shape, F32)],
        )
        sent = on_device(fold_body, (other, swap(core_sent, "row", 1)), [shape(rest, BF16)])[0]
        came = [swap(sent_own, "row", 1), swap(sent, "row", bits[1])]
    x2, g1, held = on_device(
        time_body,
        (near, near_cot, far, *centre),
        [shape(y1.shape, BF16)] * 2 + [shape((2 * ch, 2 * cols), BF16)],
    )
    slots = {k: (v,) for k, v in gather(held, "row", bits[1:]).items()}
    slots[1] = (swap(held, "row", 1),)
    for k in list(slots):
        if k > 1:
            halves = (slots[k][0][:ch], slots[k][0][ch:])
            slots[k ^ 1] = tuple(swap(v, "row", 1) for v in halves)
    gathered = [v for k in slot_order(peers) for v in slots[k]]
    count = len(gathered)

    if even:
        rows = space_rows // devices
        period, layout = segments(width)
        short = -(-rows // period)
        held_rows = round_up(short, 8)
        full = short * len(layout)
        deep = round_up(time_rows // devices + full - short + held_rows, 16)
        piece = (deep, LANES)
        scratch = (round_up(space_rows + 8 * period + rows, 8), LANES)
        pieces = on_device(
            functools.partial(space_sum_body, count, groups, rows, time_rows // devices),
            gathered,
            [shape((steps, *piece), F32)],
            [pltpu.VMEM((peers, 2 * ch, 2 * cols), BF16)] + [pltpu.VMEM(scratch, F32)] * 2,
        )
        mine, *sends = on_device(
            functools.partial(join_body, time_rows // devices, outer),
            (*pieces, kept, *came),
            [shape(piece, F32)] + [shape(piece, BF16)] * (steps - 1),
        )
        order = sorted(range(1, steps), key=lambda k: (k < steps // 2, k >= steps // 2 and k & 1, -k))
        arrived = [swap(sends[k - 1], "tm", k) for k in order]
        space_share, time_share = on_device(
            functools.partial(final_body, factor, len(layout), short),
            (mine, *arrived),
            [
                shape((held_rows * len(layout), LANES), F32),
                shape((time_rows // devices, time_width), F32),
            ],
        )
        space_share = space_share.reshape(-1)[: rows * width]
        time_share = time_share.reshape(-1)
    else:
        total = on_device(
            time_sum_whole_body, (near_cot, far, packed), [shape((time_rows, time_width), F32)]
        )[0]
        time_share = factor * lax.psum_scatter(
            total.reshape(-1), ("tm", "row"), scatter_dimension=0, tiled=True
        )
        total = on_device(
            functools.partial(space_sum_whole_body, count, groups),
            gathered,
            [shape((space_rows, width), F32)],
            [pltpu.VMEM((peers, 2 * ch, 2 * cols), BF16)],
        )[0]
        total = total.reshape(steps, peers, -1)
        total = lax.dynamic_index_in_dim(total, lax.axis_index("row"), 1, keepdims=False)
        space_share = factor * lax.psum_scatter(
            total.reshape(-1), "tm", scatter_dimension=0, tiled=True
        )

    x1, x2, g1, g2 = on_device(
        functools.partial(space_body, count),
        (*gathered, y1, c2, x2, g1, weight_space),
        [shape(y1.shape, BF16)] * 4,
        [pltpu.VMEM((peers + 2, 2 * ch, 2 * cols), BF16)],
    )
    return x1, x2, g1, g2, space_share, time_share


def solution(mesh):
    video = P("tm", "row", None, None)
    share = P(("tm", "row"))
    return jax.shard_map(
        per_device,
        mesh=mesh,
        in_specs=(video,) * 4 + (P(), P()),
        out_specs=(video,) * 4 + (share, share),
        check_vma=False,
    )
```

```python
import functools
import math

import jax
import jax.numpy as jnp
from jax import lax
from jax.experimental import pallas as pl
from jax.experimental.pallas import tpu as pltpu
from jax.sharding import PartitionSpec as P

HAAR = 0.7071067811865476
LANES = 128
F32 = jnp.float32
BF16 = jnp.bfloat16


def round_up(value, unit):
    return (value + unit - 1) // unit * unit


def on_device(body, args, outs, scratch=(), far=0):
    whole = pl.BlockSpec(memory_space=pltpu.VMEM)
    moved = sum(math.prod(a.shape) * a.dtype.itemsize for a in (*args, *outs))
    scratch = [*scratch, *(pltpu.VMEM(a.shape, a.dtype) for a in args[:far])]
    if far:
        scratch.append(pltpu.SemaphoreType.DMA((far,)))
    return pl.pallas_call(
        body,
        out_shape=outs,
        in_specs=[pl.BlockSpec(memory_space=pltpu.HBM)] * far + [whole] * (len(args) - far),
        out_specs=[whole] * len(outs),
        scratch_shapes=scratch,
        compiler_params=pltpu.CompilerParams(vmem_limit_bytes=40 * 1024 * 1024),
        cost_estimate=pl.CostEstimate(flops=0, bytes_accessed=moved, transcendentals=0),
    )(*[pltpu.with_memory_space_constraint(a, pltpu.HBM) for a in args[:far]], *args[far:])


def shape(dims, dtype):
    return jax.ShapeDtypeStruct(tuple(dims), dtype)


def sigmoid(v):
    return 1.0 / (1.0 + jnp.exp(-v))


def silu_slope(v):
    s = sigmoid(v)
    return s * (1.0 + v * (1.0 - s))


def dot(left, right, left_dim, right_dim):
    return lax.dot_general(
        left, right, (((left_dim,), (right_dim,)), ((), ())), preferred_element_type=F32
    )


def squeezed(ref):
    even, odd = ref[0, 0].astype(F32), ref[1, 0].astype(F32)
    return jnp.concatenate([(even + odd) * HAAR, (even - odd) * HAAR], axis=-1)


def unsqueezed(packed):
    half = packed.shape[-1] // 2
    low, high = packed[:, :half], packed[:, half:]
    return (low + high) * HAAR, (low - high) * HAAR


def fetch(far, near, sems):
    copies = [pltpu.make_async_copy(f, n, sems.at[i]) for i, (f, n) in enumerate(zip(far, near))]
    for copy in copies:
        copy.start()
    for copy in copies:
        copy.wait()


def open_body(y_far, cot_far, out_ref, y_ref, cot_ref, sems):
    fetch((y_far, cot_far), (y_ref, cot_ref), sems)
    sq = squeezed(y_ref)
    cols = sq.shape[0]
    out_ref[:cols] = (sq * sigmoid(sq)).astype(BF16)
    out_ref[cols:] = squeezed(cot_ref).astype(BF16)


def centre_body(y1_far, y2_far, c1_far, weight_far, own, *refs):
    (forth, back, slope, base, weight_out), (y1, y2, c1, weight, sems) = refs[:5], refs[5:]
    fetch((y1_far, y2_far, c1_far, weight_far), (y1, y2, c1, weight), sems)
    cols = own.shape[0] // 2
    groups, width = weight.shape[1:3]
    for q in range(groups):
        lanes = slice(q * width, (q + 1) * width)
        forth[:, lanes] = dot(own[:cols, lanes], weight[1, q], 1, 0)
        back[:, lanes] = dot(own[cols:, lanes], weight[1, q], 1, 1)
    slope[...] = silu_slope(squeezed(y1))
    for f in range(2):
        base[0, f] = y2[f, 0]
        base[1, f] = c1[f, 0]
    weight_out[...] = weight[...]


def time_body(near, near_cot, far, forth0, back0, slope, base, weight, x2_out, g1_out, held_out):
    cols = forth0.shape[0]
    groups, width = weight.shape[1:3]
    tap = jnp.where(lax.axis_index("tm") % 2 == 0, 2, 0)
    forth, back = [], []
    for q in range(groups):
        lanes = slice(q * width, (q + 1) * width)
        sides = jnp.concatenate([near[:cols, lanes], far[:cols, lanes]], axis=1)
        taps = jnp.concatenate([weight[tap, q], weight[2 - tap, q]], axis=0)
        forth.append(forth0[:, lanes] + dot(sides, taps, 1, 0))
        sides = jnp.concatenate([near_cot[:, lanes], far[cols:, lanes]], axis=1)
        taps = jnp.concatenate([weight[2 - tap, q], weight[tap, q]], axis=1)
        back.append(back0[:, lanes] + dot(sides, taps, 1, 1))
    branch = unsqueezed(jnp.concatenate(forth, axis=-1))
    back = unsqueezed(jnp.concatenate(back, axis=-1) * slope[...])
    acts, cots = [], []
    for f in range(2):
        x2 = (base[0, f].astype(F32) - branch[f].astype(BF16).astype(F32)).astype(BF16)
        g1 = (base[1, f].astype(F32) + back[f].astype(BF16).astype(F32)).astype(BF16)
        x2_out[f, 0] = x2
        g1_out[f, 0] = g1
        v = x2.astype(F32)
        acts.append(v * sigmoid(v))
        cots.append(g1.astype(F32))
    ch = held_out.shape[0] // 2
    held_out[:ch] = jnp.concatenate(acts, axis=0).astype(BF16).T
    held_out[ch:] = jnp.concatenate(cots, axis=0).astype(BF16).T


def time_terms(acts, pairs, total):
    width = total.shape[1]
    act = jnp.concatenate(acts, axis=0).T
    groups = act.shape[0] // width
    for k, cot in pairs:
        for q in range(groups):
            part = slice(q * width, (q + 1) * width)
            at = pl.multiple_of((k * groups + q) * width, width)
            total[pl.ds(at, width), :] = dot(act[part], cot[:, part], 1, 0)


def side_terms(near_cot, far, own, total):
    cols = far.shape[0] // 2
    tap = jnp.where(lax.axis_index("tm") % 2 == 0, 0, 2)
    time_terms([own[:cols]], ((tap, near_cot[...]), (2 - tap, far[cols:])), total)


def middle_terms(owns, total):
    cols = owns[0].shape[0] // 2
    cot = jnp.concatenate([v[cols:] for v in owns], axis=0)
    time_terms([v[:cols] for v in owns], ((1, cot),), total)


def outer_steps(steps, peers, taps, rows):
    size = steps * peers * rows // taps
    return [
        t
        for t in range(steps)
        if t * peers * rows < size or (t + 1) * peers * rows > (taps - 1) * size
    ]


def time_outer_body(rows, offset, near_cot, far, own, keep, send, total):
    me, peers, steps = lax.axis_index("row"), lax.axis_size("row"), lax.axis_size("tm")
    held, third = keep.shape[1], steps * peers * rows // 3
    total[third : 2 * third] = jnp.zeros((third, total.shape[1]), F32)
    side_terms(near_cot, far, own, total)
    for i, t in enumerate(outer_steps(steps, peers, 3, rows)):
        mine = (t * peers + (me ^ offset)) * rows
        other = (t * peers + (me ^ offset ^ 1)) * rows
        keep[i] = total[pl.ds(mine, held), :]
        send[i] = total[pl.ds(other, held), :].astype(BF16)


def time_own_body(rows, outer, *refs):
    owns, (keep, send, total) = refs[:-3], refs[-3:]
    me, peers, steps = lax.axis_index("row"), lax.axis_size("row"), lax.axis_size("tm")
    held, third = keep.shape[1], steps * peers * rows // 3
    total[:third] = outer[:third]
    total[2 * third :] = outer[2 * third :]
    middle_terms(owns, total)
    for t in range(steps):
        keep[t] = total[pl.ds((t * peers + me) * rows, held), :]
        send[t] = total[pl.ds((t * peers + (me ^ 1)) * rows, held), :].astype(BF16)


def time_sum_whole_body(near_cot, far, own, total):
    side_terms(near_cot, far, own, total)
    middle_terms((own,), total)


def fold_body(kept, came, send):
    send[...] = (kept[...] + came[...].astype(F32)).astype(BF16)


def place(slots, rows_ref, lead):
    me, ch = lax.axis_index("row"), rows_ref.shape[1]
    peers = lax.axis_size("row")
    whole = peers // 2 + 1
    rest = slots[whole:]
    parts = len(rest) // (peers - whole) if rest else 1
    slots = [(v,) for v in slots[:whole]] + [
        rest[i : i + parts] for i in range(0, len(rest), parts)
    ]
    for k, refs in zip(slot_order(peers), slots):
        for j, ref in enumerate(refs):
            size = ch // len(refs)
            rows_ref[(me ^ k) + lead, j * size : (j + 1) * size] = ref[...]


def space_terms(slots, rows_ref, cols, store):
    peers = lax.axis_size("row")
    ch = rows_ref.shape[1] // 2
    place(slots, rows_ref, 0)
    column = lax.broadcasted_iota(jnp.int32, (ch, LANES), 1) % cols
    act, shifts = [], ([], [], [])
    for r in range(peers):
        act.append(rows_ref[r, :ch])
        cot = rows_ref[r, ch:]
        wide = cot.astype(F32)
        later = jnp.where(column == cols - 1, 0.0, pltpu.roll(wide, LANES - 1, 1))
        sooner = jnp.where(column == 0, 0.0, pltpu.roll(wide, 1, 1))
        for held, value in zip(shifts, (later.astype(BF16), cot, sooner.astype(BF16))):
            held.append(value)
    for a in range(3):
        pairs = [(r, r - a + 1) for r in range(peers) if 0 <= r - a + 1 < peers]
        left = jnp.concatenate([act[r] for r, _ in pairs], axis=1)
        for b in range(3):
            right = jnp.concatenate([shifts[b][r] for _, r in pairs], axis=1)
            store(a * 3 + b, left, right)


def segments(width):
    period = LANES // math.gcd(width, LANES)
    found = []
    for j in range(period * width // LANES):
        row, lane = [], 0
        while lane < LANES:
            at = j * LANES + lane
            source, column = divmod(at, width)
            tile, first = divmod(column, LANES)
            row.append((lane, source, tile, (lane - first) % LANES))
            lane += min(LANES - first, width - column, LANES - lane)
        found.append(row)
    return period, found


def space_sum_body(count, groups, rows, time_rows, *refs):
    peers, steps = lax.axis_size("row"), lax.axis_size("tm")
    slots, refs = refs[:count], refs[count:]
    out, rows_ref, main, rest = refs
    ch = rows_ref.shape[1] // 2
    width = ch // groups

    def store(tap, left, right):
        for q in range(groups):
            part = slice(q * width, (q + 1) * width)
            term = dot(left[part], right[part], 1, 1)
            at = pl.ds((tap * groups + q) * width, width)
            main[at, :] = term[:, :LANES]
            rest[at, : width - LANES] = term[:, LANES:]

    space_terms(slots, rows_ref, LANES // 2, store)
    period, layout = segments(width)
    held = round_up(-(-rows // period), 8)
    lane = lax.broadcasted_iota(jnp.int32, (held, LANES), 1)
    here, me = lax.axis_index("tm"), lax.axis_index("row")
    short = -(-rows // period)
    for k in range(steps):
        t = here ^ k
        start = (t * peers + me) * rows
        rolled = {}

        def source(j, tile, amount):
            if (j, tile, amount) not in rolled:
                ref = (main, rest)[tile]
                value = ref[pl.ds(start + j, held, stride=period), :]
                rolled[j, tile, amount] = pltpu.roll(value, amount, 1) if amount else value
            return rolled[j, tile, amount]

        out[k, : round_up(time_rows, 8)] = jnp.zeros((round_up(time_rows, 8), LANES), F32)
        for i, row in enumerate(layout):
            value = None
            for first, j, tile, amount in row:
                piece = source(j, tile, amount)
                value = piece if value is None else jnp.where(lane < first, value, piece)
            out[k, pl.ds(time_rows + i * short, held), :] = value


def join_body(time_rows, outer, pieces, kept, core_came, came, mine, *sends):
    tall, steps = kept.shape[1], kept.shape[0]
    row = lax.broadcasted_iota(jnp.int32, (tall, LANES), 0)
    gap = steps - len(outer)
    for k in range(pieces.shape[0]):
        t = lax.axis_index("tm") ^ k
        first = next((i for i, v in enumerate(outer) if v != i), len(outer))
        over = t >= first + gap
        sent = jnp.logical_or(t < first, over)
        terms = came[jnp.where(over, t - gap, jnp.minimum(t, len(outer) - 1))].astype(F32)
        terms = kept[t] + core_came[t].astype(F32) + jnp.where(sent, terms, 0.0)
        head = pieces[k, :tall] + jnp.where(row < time_rows, terms, 0.0)
        piece = jnp.concatenate([head, pieces[k, tall:]], axis=0)
        if k == 0:
            mine[...] = piece
        else:
            sends[k - 1][...] = piece.astype(BF16)


def space_sum_whole_body(count, groups, *refs):
    slots, (total, rows_ref) = refs[:count], refs[count:]
    ch = rows_ref.shape[1] // 2
    width = ch // groups

    def store(tap, left, right):
        for q in range(groups):
            part = slice(q * width, (q + 1) * width)
            at = pl.ds((tap * groups + q) * width, width)
            total[at, :] = dot(left[part], right[part], 1, 1)

    space_terms(slots, rows_ref, LANES // 2, store)


def final_body(factor, stride, short, *refs):
    (mine, *came), (space_out, time_out) = refs[:-2], refs[-2:]
    total = mine[...]
    for ref in came:
        total = total + ref[...].astype(F32)
    total = total * factor
    first, held = time_out.shape[0], space_out.shape[0] // stride
    time_out[...] = total[:first]
    for j in range(stride):
        at = first + j * short
        space_out[pl.ds(j, held, stride=stride), :] = total[at : at + held]


def space_body(count, *refs):
    peers = lax.axis_size("row")
    slots, refs = refs[:count], refs[count:]
    y1, c2, x2, g1, weight, x1_out, x2_out, g1_out, g2_out, rows_ref = refs
    x2_out[...] = x2[...]
    g1_out[...] = g1[...]
    me = lax.axis_index("row")
    cols, ch = y1.shape[2:]
    groups, width = weight.shape[2:4]
    rows_ref[0] = jnp.zeros(rows_ref.shape[1:], BF16)
    rows_ref[peers + 1] = jnp.zeros(rows_ref.shape[1:], BF16)
    place(slots, rows_ref, 1)
    column = lax.broadcasted_iota(jnp.int32, (LANES, width), 0) % cols
    forth, back = [None] * groups, [None] * groups
    for a in range(3):
        row = rows_ref[me + a].astype(F32).T
        for q in range(groups):
            for first, sums in ((0, forth), (ch, back)):
                value = row[:, first + q * width : first + (q + 1) * width]
                sooner = jnp.where(column == 0, 0.0, pltpu.roll(value, 1, 0))
                later = jnp.where(column == cols - 1, 0.0, pltpu.roll(value, LANES - 1, 0))
                for b, moved in enumerate((sooner, value, later)):
                    if first:
                        term = dot(moved.astype(BF16), weight[2 - a, 2 - b, q], 1, 1)
                    else:
                        term = dot(moved.astype(BF16), weight[a, b, q], 1, 0)
                    sums[q] = term if sums[q] is None else sums[q] + term
    forth = jnp.concatenate(forth, axis=-1)
    back = jnp.concatenate(back, axis=-1)
    for f in range(2):
        part = slice(f * cols, (f + 1) * cols)
        x1_out[f, 0] = (y1[f, 0].astype(F32) - forth[part]).astype(BF16)
        slope = silu_slope(x2[f, 0].astype(F32))
        g2_out[f, 0] = (c2[f, 0].astype(F32) + slope * back[part]).astype(BF16)


def swap(x, axis, bit):
    return lax.ppermute(x, axis, [(i, i ^ bit) for i in range(lax.axis_size(axis))])


def gather(x, axis, bits):
    slots = {0: x}
    for bit in reversed(bits):
        for k in list(slots):
            slots[k ^ bit] = swap(slots[k], axis, bit)
    return slots


def slot_order(peers):
    last = [k for k in range(peers) if k & 1 and k > 1]
    return [k for k in range(peers) if k not in last] + last


def row_offsets(bits):
    if not bits:
        return [0]
    rest = row_offsets(bits[1:])
    return rest + [o ^ bits[0] for o in rest]


def neighbours(x, axis, first):
    lower = range(first, lax.axis_size(axis) - 1, 2)
    return lax.ppermute(x, axis, [p for i in lower for p in ((i, i + 1), (i + 1, i))])


def per_device(y1, y2, c1, c2, weight_space, temporal_weight):
    steps, peers = lax.axis_size("tm"), lax.axis_size("row")
    devices = steps * peers
    frames, rows_here, cols, ch = y1.shape
    groups = weight_space.shape[2]
    width = ch // groups
    taps = weight_space.shape[0] * weight_space.shape[1]
    factor = 1.0 / math.sqrt(frames * rows_here * cols * devices)
    time_groups, time_width = temporal_weight.shape[1:3]
    time_rows = 3 * time_groups * time_width
    space_rows = taps * ch

    packed = on_device(open_body, (y1, c2), [shape((2 * cols, 2 * ch), BF16)], far=2)[0]
    up = [(i, i + 1) for i in range(steps - 1)]
    near, far = neighbours(packed, "tm", 0), neighbours(packed, "tm", 1)
    wide = shape((cols, 2 * ch), F32)
    centre = on_device(
        centre_body,
        (y1, y2, c1, temporal_weight, packed),
        [wide] * 3 + [shape((2, 2, cols, ch), BF16), shape(temporal_weight.shape, BF16)],
        far=4,
    )

    near, centre = lax.optimization_barrier((near, centre))
    near_cot = near[cols:]
    bits = [1 << i for i in range(peers.bit_length() - 1)]
    even = time_rows % devices == 0 and space_rows % devices == 0 and peers == 4
    owns = gather(packed, "row", bits[1:]) if even else {0: packed}
    owns = [owns[k] for k in sorted(owns)]
    if even:
        rows = time_rows // devices
        tall = round_up(rows, 16)
        offsets = row_offsets(bits[1:])
        block = (steps, tall, time_width)
        outer = outer_steps(steps, peers, 3, rows)
        rest = (len(outer), *block[1:])
        table = shape((round_up(time_rows + tall, 8), time_width), F32)
        other, core_sent, table_outer = on_device(
            functools.partial(time_outer_body, rows, offsets[1]),
            (near_cot, far, packed),
            [shape(rest, F32), shape(rest, BF16), table],
        )
        kept, sent_own = on_device(
            functools.partial(time_own_body, rows),
            (table_outer, *owns),
            [shape(block, F32), shape(block, BF16)],
            [pltpu.VMEM(table.shape, F32)],
        )
        sent = on_device(fold_body, (other, swap(core_sent, "row", 1)), [shape(rest, BF16)])[0]
        came = [swap(sent_own, "row", 1), swap(sent, "row", bits[1])]
    x2, g1, held = on_device(
        time_body,
        (near, near_cot, far, *centre),
        [shape(y1.shape, BF16)] * 2 + [shape((2 * ch, 2 * cols), BF16)],
    )
    slots = {k: (v,) for k, v in gather(held, "row", bits[1:]).items()}
    slots[1] = (swap(held, "row", 1),)
    for k in list(slots):
        if k > 1:
            halves = (slots[k][0][:ch], slots[k][0][ch:])
            slots[k ^ 1] = tuple(swap(v, "row", 1) for v in halves)
    gathered = [v for k in slot_order(peers) for v in slots[k]]
    count = len(gathered)

    if even:
        rows = space_rows // devices
        period, layout = segments(width)
        short = -(-rows // period)
        held_rows = round_up(short, 8)
        full = short * len(layout)
        deep = round_up(time_rows // devices + full - short + held_rows, 16)
        piece = (deep, LANES)
        scratch = (round_up(space_rows + 8 * period + rows, 8), LANES)
        pieces = on_device(
            functools.partial(space_sum_body, count, groups, rows, time_rows // devices),
            gathered,
            [shape((steps, *piece), F32)],
            [pltpu.VMEM((peers, 2 * ch, 2 * cols), BF16)] + [pltpu.VMEM(scratch, F32)] * 2,
        )
        mine, *sends = on_device(
            functools.partial(join_body, time_rows // devices, outer),
            (*pieces, kept, *came),
            [shape(piece, F32)] + [shape(piece, BF16)] * (steps - 1),
        )
        order = sorted(range(1, steps), key=lambda k: (k < steps // 2, k >= steps // 2 and k & 1, -k))
        arrived = [swap(sends[k - 1], "tm", k) for k in order]
        space_share, time_share = on_device(
            functools.partial(final_body, factor, len(layout), short),
            (mine, *arrived),
            [
                shape((held_rows * len(layout), LANES), F32),
                shape((time_rows // devices, time_width), F32),
            ],
        )
        space_share = space_share.reshape(-1)[: rows * width]
        time_share = time_share.reshape(-1)
    else:
        total = on_device(
            time_sum_whole_body, (near_cot, far, packed), [shape((time_rows, time_width), F32)]
        )[0]
        time_share = factor * lax.psum_scatter(
            total.reshape(-1), ("tm", "row"), scatter_dimension=0, tiled=True
        )
        total = on_device(
            functools.partial(space_sum_whole_body, count, groups),
            gathered,
            [shape((space_rows, width), F32)],
            [pltpu.VMEM((peers, 2 * ch, 2 * cols), BF16)],
        )[0]
        total = total.reshape(steps, peers, -1)
        total = lax.dynamic_index_in_dim(total, lax.axis_index("row"), 1, keepdims=False)
        space_share = factor * lax.psum_scatter(
            total.reshape(-1), "tm", scatter_dimension=0, tiled=True
        )

    x1, x2, g1, g2 = on_device(
        functools.partial(space_body, count),
        (*gathered, y1, c2, x2, g1, weight_space),
        [shape(y1.shape, BF16)] * 4,
        [pltpu.VMEM((peers + 2, 2 * ch, 2 * cols), BF16)],
    )
    return x1, x2, g1, g2, space_share, time_share


def solution(mesh):
    video = P("tm", "row", None, None)
    share = P(("tm", "row"))
    return jax.shard_map(
        per_device,
        mesh=mesh,
        in_specs=(video,) * 4 + (P(), P()),
        out_specs=(video,) * 4 + (share, share),
        check_vma=False,
    )
```
